32 devices in a mesh: seq: 16 (over z, y, core), tensor: 2 (over x).
Axes of the slice: x: 2, y: 2, z: 4, core: 2. Of those that a mesh axis runs over, the one named last changes fastest.
Arguments:
- q_in: float32 [4096, 5120], P('seq', 'tensor'), may hold values from -520 to 520
- k_in: float32 [4096, 5120], P('seq', 'tensor'), may hold values from -520 to 520
- v_in: bfloat16 [4096, 5120], P('seq', 'tensor'), may hold values from -12 to 12
- q_gain: float32 [5120], P('tensor'), may hold values from 0.8 to 2
- k_gain: float32 [5120], P('tensor'), may hold values from 0.8 to 2
- frames: int32 [32], replicated, may hold values from 0 to 2, never falling along the last dimension, each value on 1 to 12 neighbouring positions
- adjacent: int32 [32, 32], P('seq'), may hold values 0 or 1
Outputs:
- attended: float32 [4096, 5120], P('seq', 'tensor')
The draws below stay inside these ranges and needn't reach their ends.
Inputs may be any that keep to these rules, and one draw needn't show every extreme that they name: `frames`: frame numbers never fall from one block to the next, and each frame spans 1 to 12 consecutive blocks.
All inputs are finite; a program needn't handle non-finite values. No bound on the sum of `adjacent` on one device may be relied on, other than what follows from the above.
Results may differ from the reference program's by a relative error of at most 0.012.
The reference program's roundings to bfloat16 on the way (of `q_norm`, `k_norm` and `rounded_weights`) count: a program that leaves them out, or rounds other values in their place, can miss the bound.
Values may be sent and summed in bfloat16 or wider, within the bound.
No kernel may reach another device: no remote copies, remote signals or barrier semaphores. Data moves between devices by JAX's collectives and lax.ppermute only.
A program may use at most 128 MiB of HBM per device.

```python
import math
import jax
import jax.numpy as jnp
import numpy as np
from jax import lax

D = 5120
HEAD_DIM = 128
TOK_DEV = 256
BLOCK = 128
FRAME_BLK = 12
BLOCKS_DEV = 2
BLOCKS = 32
TOKENS = 4096
FRAMES = 3
REACH = 12
N_SEQ = 16


def drawn_input(key, role_index):
    own_key = jax.random.fold_in(key, 101 + role_index)
    split_keys = jax.random.split(own_key, 3)
    scale_top = math.log(10.0)
    entries = jnp.clip(jax.random.normal(split_keys[2], (TOKENS, D), jnp.float32), -4.0, 4.0)
    row_scales = jnp.exp(jax.random.uniform(split_keys[0], (TOKENS, 1), jnp.float32, 0.0, scale_top))
    rising = jnp.exp(jnp.arange(D, dtype=jnp.float32) * (math.log(3.0) / (D - 1)))
    col_scales = jnp.exp(jax.random.uniform(split_keys[1], (1, D), jnp.float32, 0.0, math.log(10.0))) * rising[None, :] / 3.0
    shaped = entries * col_scales
    drawn = shaped * row_scales
    return drawn


def draw_q_in(key, part):
    return drawn_input(key, 0)


def draw_k_in(key, part):
    return drawn_input(key, 1)


def place_ends(array, key, low, top_value):
    longest = array.shape.index(max(array.shape))
    spots = []
    for shift in (0, 1):
        where = [jax.random.randint(jax.random.fold_in(key, axis), (), 0, length) for axis, length in enumerate(array.shape)]
        where[longest] = (where[longest] + shift) % array.shape[longest]
        spots.append(tuple(where))
    return array.at[spots[0]].set(low).at[spots[1]].set(top_value)


def levels(key, dims, shards, smallest, high):
    level, own = 1.0, jax.random.fold_in(key, 6)
    for position, blocks in shards:
        draws = jnp.exp(jax.random.uniform(jax.random.fold_in(own, position), (blocks,), jnp.float32, smallest / len(shards), high / len(shards)))
        level = level * jnp.repeat(draws, dims[position] // blocks).reshape([-1 if axis == position else 1 for axis in range(len(dims))])
    return level


def split_up(count, total, limit, lean):
    weights = [(1 << 20) // math.isqrt(rank ** lean) + 1 for rank in range(2, count + 1)]
    spare, counts = total - limit - (count - 1), [1] * (count - 1)
    while spare > 0:
        free = [i for i in range(count - 1) if counts[i] < limit]
        whole, left = sum([weights[i] for i in free]), spare
        for i in free:
            extra = min(limit - counts[i], max(1, left * weights[i] // whole), spare)
            counts[i] = counts[i] + extra
            spare = spare - extra
    return np.array([limit] + counts)


def uneven_parts(key, number_of, total, most, slope):
    if number_of == 2:
        one = jax.random.randint(key, (), max(1, total - most), min(most, total - 1) + 1)
        return jnp.stack([one, total - one])
    lengths = jnp.asarray(split_up(number_of, total, most, slope), jnp.int32)
    pairs = (number_of - 1) // 2
    source_of, taker = lengths[1:1 + 2 * pairs:2], lengths[2:2 + 2 * pairs:2]
    room = jnp.minimum(source_of - 1, most - taker)
    moved = jax.random.randint(jax.random.fold_in(key, 1), (pairs,), 0, 1 << 20) % (room + 1)
    lengths = lengths.at[1:1 + 2 * pairs:2].set(source_of - moved).at[2:2 + 2 * pairs:2].set(taker + moved)
    return lengths[jax.random.permutation(jax.random.fold_in(key, 2), number_of)]


def bell_draw(key, extent, spread, bound, cuts=(), kind=jnp.bfloat16):
    values = jax.random.normal(key, extent, jnp.float32) * spread
    if len(cuts) > 0:
        values = levels(key, extent, cuts, -0.22, 0.18) * values
    return jnp.clip(values, min=-bound, max=bound).astype(kind)


def setup_inputs(seed: int = 0) -> dict:
    key_list = jax.random.split(jax.random.key(seed), 8)
    q_in = draw_q_in(jax.random.fold_in(key_list[7], 71), 0)
    k_in = draw_k_in(jax.random.fold_in(key_list[7], 71), 0)
    v_in = bell_draw(key_list[2], (TOKENS, D), 2.0, 12.0, ((0, 16), (1, 2)))
    q_gain = jnp.clip(0.8 + 1.2 * jax.random.uniform(key_list[3], (D,), jnp.float32) ** levels(key_list[3], (D,), ((0, 2),), -0.2, 0.2), 0.8, 2.0)
    k_gain = jnp.clip(0.8 + 1.2 * jax.random.uniform(key_list[4], (D,), jnp.float32) ** levels(key_list[4], (D,), ((0, 2),), -0.2, 0.2), 0.8, 2.0)
    frames = jnp.searchsorted(jnp.cumsum(uneven_parts(key_list[5], FRAMES, BLOCKS, FRAME_BLK, 0)), jnp.arange(BLOCKS), side="right").astype(jnp.int32)
    adjacent = place_ends((jax.random.randint(key_list[6], (BLOCKS, BLOCKS), 0, 2) < 1).astype(jnp.int32), jax.random.fold_in(key_list[6], 1), 0, 1)
    return {"q_in": q_in, "k_in": k_in, "v_in": v_in, "q_gain": q_gain, "k_gain": k_gain, "frames": frames, "adjacent": adjacent}


epsilon = 1e-06
blocked = -1e+30

def normalized(inputs, gain_row):
    return (inputs / jnp.sqrt(lax.optimization_barrier(jnp.mean(inputs * inputs, axis=1, keepdims=True)) + epsilon) * gain_row).astype(jnp.bfloat16)

def reference(q_in, k_in, v_in, q_gain, k_gain, frames, adjacent):
    q_norm = normalized(q_in, q_gain)
    k_norm = normalized(k_in, k_gain)
    head_count = D // HEAD_DIM
    margin = REACH * TOK_DEV
    window = (2 * REACH + 1) * TOK_DEV
    window_blocks = (2 * REACH + 1) * BLOCKS_DEV
    margin_blocks = REACH * BLOCKS_DEV
    padded_keys = jnp.pad(k_norm, ((margin, margin), (0, 0)))
    padded_values = jnp.pad(v_in, ((margin, margin), (0, 0)))
    padded_frames = jnp.pad(frames, (margin_blocks, margin_blocks), constant_values=-1000)
    padded_adjacent = jnp.pad(adjacent, ((0, 0), (margin_blocks, margin_blocks)))
    score_scale = 1.0 / math.sqrt(HEAD_DIM)

    def one_device(device):
        first_row = (device * TOK_DEV).astype(jnp.int32)
        first_block = (device * BLOCKS_DEV).astype(jnp.int32)
        queries = lax.dynamic_slice_in_dim(q_norm, first_row, TOK_DEV, 0).astype(jnp.float32).reshape(TOK_DEV, head_count, HEAD_DIM)
        key_rows = lax.dynamic_slice_in_dim(padded_keys, first_row, window, 0).astype(jnp.float32).reshape(window, head_count, HEAD_DIM)
        value_rows = lax.dynamic_slice_in_dim(padded_values, first_row, window, 0).astype(jnp.float32).reshape(window, head_count, HEAD_DIM)
        query_frames = lax.dynamic_slice_in_dim(frames, first_block, BLOCKS_DEV, 0)
        key_frames = lax.dynamic_slice_in_dim(padded_frames, first_block, window_blocks, 0)
        adjacent_rows = lax.dynamic_slice(padded_adjacent, (first_block, first_block), (BLOCKS_DEV, window_blocks))
        frame_gap = jnp.abs(query_frames[:, None] - key_frames[None, :])
        allowed = (frame_gap == 0) | (frame_gap == 1) & (adjacent_rows == 1)
        scores = jnp.einsum('thd,uhd->htu', queries, key_rows, precision=lax.Precision.HIGHEST) * score_scale
        tiled_scores = scores.reshape(head_count, BLOCKS_DEV, BLOCK, window_blocks, BLOCK)
        tiled_scores = jnp.where(allowed[None, :, None, :, None], tiled_scores, blocked)
        scores = tiled_scores.reshape(head_count, TOK_DEV, window)
        row_max = lax.optimization_barrier(jnp.max(scores, axis=2, keepdims=True))
        weights = jnp.exp(scores - row_max)
        row_total = lax.optimization_barrier(jnp.sum(weights, axis=2))
        rounded_weights = weights.astype(jnp.bfloat16).astype(jnp.float32)
        mixed_sum = jnp.einsum('htu,uhd->thd', rounded_weights, value_rows, precision=lax.Precision.HIGHEST)
        return (mixed_sum / row_total.T[:, :, None]).reshape(TOK_DEV, D)
    results = lax.map(one_device, jnp.arange(N_SEQ, dtype=jnp.int32))
    return results.reshape(TOKENS, D)
```

```python
import functools
import math

import jax
import jax.numpy as jnp
from jax import lax
from jax.experimental import pallas as pl
from jax.experimental.pallas import tpu as pltpu
from jax.sharding import PartitionSpec as P

HEAD_DIM = 128
BLOCK = 128
epsilon = 1e-06
blocked = -1e30
GROUP = 4
MIB = 1024 * 1024


def value_pieces_kernel(place_ref, v_ref, *outs, groups, chunks):
    per_group = sum(chunks)
    for shift in range(groups):
        group = lax.rem(place_ref[0] + shift, groups)
        first = 0
        for c, heads in enumerate(chunks):
            out = outs[c * groups + shift]
            for h in range(heads):
                column = pl.multiple_of((group * per_group + first + h) * HEAD_DIM, HEAD_DIM)
                out[h] = v_ref[:, pl.ds(column, HEAD_DIM)]
            first += heads


def square_sums_kernel(q_ref, k_ref, out_ref):
    q, k = q_ref[...], k_ref[...]
    out_ref[:, 0:1] = jnp.sum(q * q, axis=1, keepdims=True)
    out_ref[:, 1:2] = jnp.sum(k * k, axis=1, keepdims=True)


def norm_pieces_kernel(
    place_ref, sums_ref, q_ref, k_ref, q_gain_ref, k_gain_ref, *outs, groups, chunks, full_width
):
    per_group = sum(chunks)
    count = groups * len(chunks)
    for role, (x_ref, gain_ref) in enumerate(((q_ref, q_gain_ref), (k_ref, k_gain_ref))):
        mean = sums_ref[:, role : role + 1] / full_width
        inverse = 1.0 / jnp.sqrt(mean + epsilon)
        for shift in range(groups):
            group = lax.rem(place_ref[0] + shift, groups)
            first = 0
            for c, heads in enumerate(chunks):
                out = outs[role * count + c * groups + shift]
                for h in range(heads):
                    column = pl.multiple_of((group * per_group + first + h) * HEAD_DIM, HEAD_DIM)
                    x = x_ref[:, pl.ds(column, HEAD_DIM)]
                    gain = gain_ref[:, pl.ds(column, HEAD_DIM)]
                    out[h] = (x * inverse * gain).astype(jnp.bfloat16)
                first += heads


def attend_kernel(count_ref, list_ref, *refs, groups, layers, blk_dev, scale):
    q_refs = refs[:groups]
    k_refs = refs[groups : groups + layers]
    v_refs = refs[groups + layers : groups + 2 * layers]
    outs = refs[groups + 2 * layers : 2 * groups + 2 * layers]
    k_all, v_all, scores = refs[2 * groups + 2 * layers :]
    for layer in range(layers):
        for g in range(groups):
            for b in range(blk_dev):
                slot = (layer * groups + g) * blk_dev + b
                rows = pl.ds(b * BLOCK, BLOCK)
                k_all[slot] = k_refs[layer][g, 0, rows, :]
                v_all[slot] = v_refs[layer][g, 0, rows, :]
    for g in range(groups):
        for b in range(blk_dev):
            query = g * blk_dev + b
            rows = pl.ds(b * BLOCK, BLOCK)
            q = q_refs[g][0, rows, :]
            count = count_ref[query]
            steps = lax.div(count + GROUP - 1, GROUP)

            def score_step(step, top):
                for u in range(GROUP):
                    spot = step * GROUP + u
                    block = lax.dot_general(
                        q,
                        k_all[list_ref[query, spot]],
                        (((1,), (1,)), ((), ())),
                        preferred_element_type=jnp.float32,
                    )
                    block = block + jnp.where(spot < count, 0.0, blocked)
                    scores[spot] = block
                    top = jnp.maximum(top, block)
                return top

            top = lax.fori_loop(
                0, steps, score_step, jnp.full((BLOCK, BLOCK), blocked, jnp.float32)
            )
            row_max = jnp.max(top, axis=1, keepdims=True)

            def weigh_step(step, current):
                total, mixed = current
                for u in range(GROUP):
                    spot = step * GROUP + u
                    weights = jnp.exp2((scores[spot] - row_max) * scale)
                    total = total + weights
                    mixed = mixed + jnp.dot(
                        weights.astype(jnp.bfloat16),
                        v_all[list_ref[query, spot]],
                        preferred_element_type=jnp.float32,
                    )
                return total, mixed

            zero = jnp.zeros((BLOCK, BLOCK), jnp.float32)
            total, mixed = lax.fori_loop(0, steps, weigh_step, (zero, zero))
            outs[g][0, rows, :] = (mixed / jnp.sum(total, axis=1, keepdims=True)).astype(
                jnp.bfloat16
            )


def collect_kernel(place_ref, *refs, groups, chunks):
    out = refs[-1]
    per_group = sum(chunks)
    for shift in range(groups):
        group = lax.rem(place_ref[0] + shift, groups)
        first = 0
        for c, heads in enumerate(chunks):
            piece = refs[c * groups + shift]
            for h in range(heads):
                column = pl.multiple_of((group * per_group + first + h) * HEAD_DIM, HEAD_DIM)
                out[:, pl.ds(column, HEAD_DIM)] = piece[h].astype(jnp.float32)
            first += heads


VMEM = pl.BlockSpec(memory_space=pltpu.VMEM)
SMEM = pl.BlockSpec(memory_space=pltpu.SMEM)


def exchanged(q_in, k_in, v_in, q_gain, k_gain, frames, adjacent, *, groups, chunks):
    rows, width = q_in.shape
    devices = lax.axis_size("seq")
    tensors = lax.axis_size("tensor")
    layers = devices // groups
    blk_dev = rows // BLOCK
    blocks = devices * blk_dev
    full_width = width * tensors
    me = lax.axis_index("seq")
    place, spot = me // layers, lax.rem(me, layers)
    place_row = place.reshape(1).astype(jnp.int32)
    f32, bf16 = jnp.float32, jnp.bfloat16
    params = pltpu.CompilerParams(vmem_limit_bytes=48 * MIB)

    def rotated(x, shift):
        pairs = [
            (z * layers + r, (z + shift) % groups * layers + r)
            for z in range(groups)
            for r in range(layers)
        ]
        return lax.ppermute(x, "seq", pairs)

    def swapped(x, bit):
        return lax.ppermute(x, "seq", [(i, i ^ bit) for i in range(devices)])

    def piece_shapes(times):
        return [
            jax.ShapeDtypeStruct((heads, rows, HEAD_DIM), bf16)
            for _ in range(times)
            for heads in chunks
            for _ in range(groups)
        ]

    def split(pieces):
        return [pieces[c * groups : (c + 1) * groups] for c in range(len(chunks))]

    v_pieces = pl.pallas_call(
        functools.partial(value_pieces_kernel, groups=groups, chunks=chunks),
        out_shape=piece_shapes(1),
        in_specs=[SMEM, VMEM],
        out_specs=[VMEM] * (groups * len(chunks)),
        compiler_params=params,
        name="value_pieces",
    )(place_row, v_in)

    sums = pl.pallas_call(
        square_sums_kernel,
        out_shape=jax.ShapeDtypeStruct((rows, 2), f32),
        in_specs=[VMEM, VMEM],
        out_specs=VMEM,
        compiler_params=params,
        name="square_sums",
    )(q_in, k_in)
    if tensors == 2:
        sums = sums + lax.ppermute(sums, "tensor", [(0, 1), (1, 0)])
    else:
        sums = lax.psum(sums, "tensor")

    normed = pl.pallas_call(
        functools.partial(
            norm_pieces_kernel, groups=groups, chunks=chunks, full_width=float(full_width)
        ),
        out_shape=piece_shapes(2),
        in_specs=[SMEM] + [VMEM] * 5,
        out_specs=[VMEM] * (2 * groups * len(chunks)),
        compiler_params=params,
        name="norm_pieces",
    )(place_row, sums, q_in, k_in, q_gain.reshape(1, width), k_gain.reshape(1, width))
    q_pieces, k_pieces = normed[: len(normed) // 2], normed[len(normed) // 2 :]

    everyone = lax.all_gather(adjacent, "seq", axis=0, tiled=True)
    gap = jnp.abs(frames[:, None] - frames[None, :])
    allowed = (gap == 0) | (gap == 1) & (everyone == 1)
    z_order = lax.rem(place - jnp.arange(groups) + groups, groups)
    query_blocks = (
        (z_order[:, None] * layers + spot) * blk_dev + jnp.arange(blk_dev)[None, :]
    ).reshape(-1)
    layer_order = jnp.bitwise_xor(spot, jnp.arange(layers))
    key_blocks = (
        (z_order[None, :, None] * layers + layer_order[:, None, None]) * blk_dev
        + jnp.arange(blk_dev)[None, None, :]
    ).reshape(-1)
    query_hot = (query_blocks[:, None] == jnp.arange(blocks)[None, :]).astype(f32)
    key_hot = (key_blocks[:, None] == jnp.arange(blocks)[None, :]).astype(f32)
    table = (query_hot @ allowed.astype(f32) @ key_hot.T) > 0.5
    upto = jnp.tril(jnp.ones((blocks, blocks), f32)).T
    position = (table.astype(f32) @ upto).astype(jnp.int32) - 1
    counts = jnp.sum(table, axis=1).astype(jnp.int32)
    spots = jnp.arange(blocks + GROUP, dtype=jnp.int32)
    chosen = table[:, :, None] & (position[:, :, None] == spots[None, None, :])
    lists = jnp.sum(
        jnp.where(chosen, jnp.arange(blocks, dtype=jnp.int32)[None, :, None], 0), axis=1
    ).astype(jnp.int32)

    scale = math.log2(math.e) / math.sqrt(HEAD_DIM)
    outputs = []
    for c, heads in enumerate(chunks):
        v_z, k_z, q_z = [
            [pieces[0]] + [rotated(pieces[s], s) for s in range(1, groups)]
            for pieces in (split(v_pieces)[c], split(k_pieces)[c], split(q_pieces)[c])
        ]
        gathered = []
        for pieces in (k_z, v_z):
            parts = {0: jnp.stack(pieces)}
            bit = layers // 2
            while bit:
                for have in list(parts):
                    parts[have ^ bit] = swapped(parts[have], bit)
                bit //= 2
            gathered.append([parts[i] for i in range(layers)])
        big = pl.BlockSpec((groups, 1, rows, HEAD_DIM), lambda h, *_: (0, h, 0, 0))
        small = pl.BlockSpec((1, rows, HEAD_DIM), lambda h, *_: (h, 0, 0))
        pairs = blocks * groups * blk_dev
        attended = pl.pallas_call(
            functools.partial(
                attend_kernel, groups=groups, layers=layers, blk_dev=blk_dev, scale=scale
            ),
            grid_spec=pltpu.PrefetchScalarGridSpec(
                num_scalar_prefetch=2,
                grid=(heads,),
                in_specs=[small] * groups + [big] * (2 * layers),
                out_specs=[small] * groups,
                scratch_shapes=[
                    pltpu.VMEM((blocks, BLOCK, HEAD_DIM), bf16),
                    pltpu.VMEM((blocks, BLOCK, HEAD_DIM), bf16),
                    pltpu.VMEM((blocks + GROUP, BLOCK, BLOCK), f32),
                ],
            ),
            out_shape=[jax.ShapeDtypeStruct((heads, rows, HEAD_DIM), bf16)] * groups,
            compiler_params=params,
            cost_estimate=pl.CostEstimate(
                flops=heads * pairs * 4 * BLOCK**3,
                bytes_accessed=heads * blocks * BLOCK * HEAD_DIM * 5,
                transcendentals=heads * pairs * BLOCK**2,
            ),
            name=f"attend_{c}",
        )(counts, lists, *q_z, *gathered[0], *gathered[1])
        outputs += [attended[0]] + [
            rotated(attended[s], groups - s) for s in range(1, groups)
        ]

    return pl.pallas_call(
        functools.partial(collect_kernel, groups=groups, chunks=chunks),
        out_shape=jax.ShapeDtypeStruct((rows, width), f32),
        in_specs=[SMEM] + [VMEM] * (groups * len(chunks)),
        out_specs=VMEM,
        compiler_params=params,
        name="collect",
    )(place_row, *outputs)


def normalized(inputs, gain_row, square_sum, full_width):
    return (inputs / jnp.sqrt(square_sum / full_width + epsilon)[:, None] * gain_row).astype(
        jnp.bfloat16
    )


def shards(q_in, k_in, v_in, q_gain, k_gain, frames, adjacent):
    tok_rows = q_in.shape[0]
    width_dev = q_in.shape[1]
    full_width = width_dev * lax.axis_size("tensor")
    q_sum, k_sum = lax.psum((jnp.sum(q_in * q_in, axis=1), jnp.sum(k_in * k_in, axis=1)), "tensor")
    q_norm = normalized(q_in, q_gain, q_sum, full_width)
    k_norm = normalized(k_in, k_gain, k_sum, full_width)
    blk_dev = tok_rows // BLOCK
    device = lax.axis_index("seq")
    first_block = device * blk_dev
    query_frames = lax.dynamic_slice_in_dim(frames, first_block, blk_dev, 0)
    score_scale = 1.0 / math.sqrt(HEAD_DIM)
    head_count = width_dev // HEAD_DIM
    q_three = q_norm.reshape(tok_rows, head_count, HEAD_DIM)

    def masked_scores(key_rows, key_start):
        key_block = key_start // BLOCK
        key_frames = lax.dynamic_slice_in_dim(frames, key_block, blk_dev, 0)
        adjacent_rows = lax.dynamic_slice_in_dim(adjacent, key_block, blk_dev, 1)
        frame_gap = jnp.abs(query_frames[:, None] - key_frames[None, :])
        allowed_here = (frame_gap == 0) | (frame_gap == 1) & (adjacent_rows == 1)
        key_three = key_rows.reshape(tok_rows, head_count, HEAD_DIM)
        raw_scores = (
            jnp.einsum("thd,uhd->htu", q_three, key_three, preferred_element_type=jnp.float32)
            * score_scale
        )
        tiled_scores = raw_scores.reshape(head_count, blk_dev, BLOCK, blk_dev, BLOCK)
        tiled_scores = jnp.where(allowed_here[None, :, None, :, None], tiled_scores, blocked)
        return tiled_scores.reshape(head_count, tok_rows, tok_rows)

    piece = lax.all_gather(k_norm, "seq", axis=0, tiled=True)
    shard_count = piece.shape[0] // tok_rows

    def one_shard(shard, current):
        key_rows = lax.dynamic_slice_in_dim(piece, shard * tok_rows, tok_rows, 0)
        return jnp.maximum(current, jnp.max(masked_scores(key_rows, shard * tok_rows), axis=2))

    row_max = lax.fori_loop(
        0, shard_count, one_shard, jnp.full((head_count, tok_rows), blocked, jnp.float32)
    )
    start_sums = (
        jnp.zeros((head_count, tok_rows), jnp.float32),
        jnp.zeros((tok_rows, head_count, HEAD_DIM), jnp.float32),
    )
    key_piece = lax.all_gather(k_norm, "seq", axis=0, tiled=True)
    value_piece = lax.all_gather(v_in, "seq", axis=0, tiled=True)
    shard_count = key_piece.shape[0] // tok_rows

    def one_shard(shard, current):
        totals, accumulated = current
        key_rows = lax.dynamic_slice_in_dim(key_piece, shard * tok_rows, tok_rows, 0)
        value_rows = lax.dynamic_slice_in_dim(value_piece, shard * tok_rows, tok_rows, 0).reshape(
            tok_rows, head_count, HEAD_DIM
        )
        weights = jnp.exp(masked_scores(key_rows, shard * tok_rows) - row_max[:, :, None])
        totals = totals + jnp.sum(weights, axis=2)
        accumulated = accumulated + jnp.einsum(
            "htu,uhd->thd",
            weights.astype(jnp.bfloat16),
            value_rows,
            preferred_element_type=jnp.float32,
        )
        return (totals, accumulated)

    totals, accumulated = lax.fori_loop(0, shard_count, one_shard, start_sums)
    return (accumulated / totals.T[:, :, None]).reshape(tok_rows, width_dev)


def plan(mesh, heads):
    devices = mesh.shape["seq"]
    for layers in (4,):
        groups = devices // layers
        if devices % layers == 0 and groups > 1 and heads % groups == 0:
            return groups
    return None


def solution(mesh):
    def step(q_in, k_in, v_in, q_gain, k_gain, frames, adjacent):
        heads = q_in.shape[1] // mesh.shape["tensor"] // HEAD_DIM
        groups = plan(mesh, heads)
        if groups is None:
            body = shards
        else:
            per_group = heads // groups
            chunks = (per_group - per_group // 2, per_group // 2)
            body = functools.partial(exchanged, groups=groups, chunks=chunks)
        return jax.shard_map(
            body,
            mesh=mesh,
            in_specs=(
                P("seq", "tensor"),
                P("seq", "tensor"),
                P("seq", "tensor"),
                P("tensor"),
                P("tensor"),
                P(),
                P("seq", None),
            ),
            out_specs=P("seq", "tensor"),
            check_vma=False,
        )(q_in, k_in, v_in, q_gain, k_gain, frames, adjacent)

    return step
```

```python
import functools
import math

import jax
import jax.numpy as jnp
from jax import lax
from jax.experimental import pallas as pl
from jax.experimental.pallas import tpu as pltpu
from jax.sharding import PartitionSpec as P

HEAD_DIM = 128
BLOCK = 128
epsilon = 1e-06
blocked = -1e30
MASK_ROWS = 16
MIB = 1024 * 1024
VMEM = pl.BlockSpec(memory_space=pltpu.VMEM)
SMEM = pl.BlockSpec(memory_space=pltpu.SMEM)
ANY = pl.BlockSpec(memory_space=pl.ANY)


def column_of(place_ref, shift, head, groups, per_group):
    group = lax.rem(place_ref[0] + shift, groups)
    return pl.multiple_of((group * per_group + head) * HEAD_DIM, HEAD_DIM)


def value_kernel(place_ref, v_ref, mask_ref, *outs, per_group):
    groups = len(outs)
    rows = v_ref.shape[0]
    for shift, out in enumerate(outs):
        for head in range(per_group):
            column = column_of(place_ref, shift, head, groups, per_group)
            out[head * rows : (head + 1) * rows, :] = v_ref[:, pl.ds(column, HEAD_DIM)]
        out[per_group * rows :, :] = mask_ref[...]


def square_sums_kernel(q_ref, k_ref, out_ref):
    q, k = q_ref[...], k_ref[...]
    out_ref[:, 0:1] = jnp.sum(q * q, axis=1, keepdims=True)
    out_ref[:, 1:2] = jnp.sum(k * k, axis=1, keepdims=True)


def normed_columns(x_ref, inverse, gain_ref, column):
    here = pl.ds(column, HEAD_DIM)
    return (x_ref[:, here] * inverse * gain_ref[:, here]).astype(jnp.bfloat16)


def key_kernel(place_ref, sums_ref, k_ref, gain_ref, *outs, per_group, full_width):
    groups = len(outs)
    rows = k_ref.shape[0]
    inverse = 1.0 / jnp.sqrt(sums_ref[:, 1:2] / full_width + epsilon)
    for shift, out in enumerate(outs):
        for head in range(per_group):
            column = column_of(place_ref, shift, head, groups, per_group)
            x = normed_columns(k_ref, inverse, gain_ref, column)
            for b in range(rows // BLOCK):
                low = head * rows + b * HEAD_DIM
                out[low : low + HEAD_DIM, :] = x[b * BLOCK : (b + 1) * BLOCK].T


def query_kernel(place_ref, sums_ref, q_ref, gain_ref, _, *outs, per_group, full_width):
    groups = len(outs)
    rows = q_ref.shape[0]
    inverse = 1.0 / jnp.sqrt(sums_ref[:, 0:1] / full_width + epsilon)
    for shift, out in enumerate(outs):
        for head in range(per_group):
            column = column_of(place_ref, shift, head, groups, per_group)
            out[head * rows : (head + 1) * rows, :] = normed_columns(
                q_ref, inverse, gain_ref, column
            )


def attend_kernel(bias_ref, q_ref, *refs, slot_of_queries, groups, layers, scale):
    k_refs, v_refs = refs[:layers], refs[layers : 2 * layers]
    out, scores = refs[-2:]
    rows = q_ref.shape[0]
    blk = rows // BLOCK
    slots = groups * layers
    q = q_ref[...]
    top = jnp.full((rows, BLOCK), blocked, jnp.float32)
    for slot in range(slots):
        keys = k_refs[slot // groups][slot % groups]
        for b in range(blk):
            block = jnp.dot(
                q, keys[b * HEAD_DIM : (b + 1) * HEAD_DIM], preferred_element_type=jnp.float32
            )
            first = (slot_of_queries * slots + slot) * blk
            block = jnp.concatenate(
                [
                    block[a * BLOCK : (a + 1) * BLOCK] + bias_ref[(first + a) * blk + b]
                    for a in range(blk)
                ],
                axis=0,
            )
            scores[slot, :, b * BLOCK : (b + 1) * BLOCK] = block
            top = jnp.maximum(top, block)
    row_max = jnp.max(top, axis=1, keepdims=True)
    total = mixed = jnp.zeros((rows, BLOCK), jnp.float32)
    for slot in range(slots):
        weights = jnp.exp2((scores[slot] - row_max) * scale)
        for b in range(blk):
            total = total + weights[:, b * BLOCK : (b + 1) * BLOCK]
        mixed = mixed + jnp.dot(
            weights.astype(jnp.bfloat16),
            v_refs[slot // groups][slot % groups],
            preferred_element_type=jnp.float32,
        )
    out[...] = (mixed / jnp.sum(total, axis=1, keepdims=True)).astype(jnp.bfloat16)


def collect_kernel(place_ref, *refs, per_group):
    out = refs[-1]
    groups = len(refs) - 1
    rows = out.shape[0]
    for shift in range(groups):
        for head in range(per_group):
            column = column_of(place_ref, shift, head, groups, per_group)
            piece = refs[shift][head * rows : (head + 1) * rows, :]
            out[:, pl.ds(column, HEAD_DIM)] = piece.astype(jnp.float32)


def exchanged(q_in, k_in, v_in, q_gain, k_gain, frames, adjacent, *, groups):
    rows, width = q_in.shape
    devices = lax.axis_size("seq")
    tensors = lax.axis_size("tensor")
    layers = devices // groups
    blk = rows // BLOCK
    blocks = devices * blk
    per_group = width // HEAD_DIM // groups
    me = lax.axis_index("seq")
    place, spot = me // layers, lax.rem(me, layers)
    place_row = place.reshape(1).astype(jnp.int32)
    f32, bf16 = jnp.float32, jnp.bfloat16
    params = pltpu.CompilerParams(vmem_limit_bytes=48 * MIB)
    def rotated(x, shift):
        pairs = [
            (z * layers + r, (z + shift) % groups * layers + r)
            for z in range(groups)
            for r in range(layers)
        ]
        return lax.ppermute(x, "seq", pairs)

    def exchange(pieces):
        return [pieces[0]] + [rotated(pieces[s], s) for s in range(1, groups)]

    def swapped(x, bit):
        return lax.ppermute(x, "seq", [(i, i ^ bit) for i in range(devices)])

    own_frames = lax.dynamic_slice_in_dim(frames, me * blk, blk, 0)
    gap = jnp.abs(own_frames[:, None] - frames[None, :])
    allowed = ((gap == 0) | (gap == 1) & (adjacent == 1)).astype(bf16)
    mask_rows = jnp.pad(allowed, ((0, MASK_ROWS - blk), (0, BLOCK - blocks)))

    v_pieces = pl.pallas_call(
        functools.partial(value_kernel, per_group=per_group),
        out_shape=[jax.ShapeDtypeStruct((per_group * rows + MASK_ROWS, HEAD_DIM), bf16)] * groups,
        in_specs=[SMEM, VMEM, VMEM],
        out_specs=[VMEM] * groups,
        compiler_params=params,
        name="value_pieces",
    )(place_row, v_in, mask_rows)
    q_in, k_in, v_pieces = lax.optimization_barrier((q_in, k_in, v_pieces))
    sums = pl.pallas_call(
        square_sums_kernel,
        out_shape=jax.ShapeDtypeStruct((rows, 2), f32),
        in_specs=[VMEM, VMEM],
        out_specs=VMEM,
        compiler_params=params,
        name="square_sums",
    )(q_in, k_in)
    v_arrived = exchange(v_pieces)
    if tensors == 2:
        sums = sums + lax.ppermute(sums, "tensor", [(0, 1), (1, 0)])
    else:
        sums = lax.psum(sums, "tensor")

    normed = dict(per_group=per_group, full_width=float(width * tensors))
    k_arrived = exchange(
        pl.pallas_call(
            functools.partial(key_kernel, **normed),
            out_shape=[jax.ShapeDtypeStruct((per_group * rows, HEAD_DIM), bf16)] * groups,
            in_specs=[SMEM] + [VMEM] * 3,
            out_specs=[VMEM] * groups,
            compiler_params=params,
            name="key_pieces",
        )(place_row, sums, k_in, k_gain.reshape(1, width))
    )
    v_stack = jnp.stack([x[: per_group * rows] for x in v_arrived])
    q_arrived = exchange(
        pl.pallas_call(
            functools.partial(query_kernel, **normed),
            out_shape=[jax.ShapeDtypeStruct((per_group * rows, HEAD_DIM), bf16)] * groups,
            in_specs=[SMEM] + [VMEM] * 3 + [ANY],
            out_specs=[VMEM] * groups,
            compiler_params=params,
            name="query_pieces",
        )(place_row, sums, q_in, q_gain.reshape(1, width), v_stack)
    )

    def spread(parts, bit):
        return parts | {have ^ bit: swapped(part, bit) for have, part in parts.items()}

    bits = [1 << i for i in reversed(range(layers.bit_length() - 1))]
    values, keys = {0: v_stack}, {}
    for bit in bits:
        values = spread(values, bit)
        if bit == bits[0]:
            k_arrived, values = lax.optimization_barrier((k_arrived, values))
            keys = {0: jnp.stack(k_arrived)}
    for bit in bits:
        keys = spread(keys, bit)
        if bit == bits[0]:
            q_arrived, keys = lax.optimization_barrier((q_arrived, keys))
    values = [values[i] for i in range(layers)]
    keys = [keys[i] for i in range(layers)]

    low = per_group * rows
    known = jnp.stack([x[low : low + blk, :blocks] for x in v_arrived]).astype(f32)
    z_order = lax.rem(place - jnp.arange(groups) + groups, groups)
    layer_order = jnp.bitwise_xor(spot, jnp.arange(layers))
    key_blocks = (
        (z_order[None, :, None] * layers + layer_order[:, None, None]) * blk
        + jnp.arange(blk)[None, None, :]
    ).reshape(-1)
    key_hot = (key_blocks[:, None] == jnp.arange(blocks)[None, :]).astype(f32)
    table = jnp.einsum("gab,kb->gak", known, key_hot).reshape(groups, blk, devices, blk)
    bias = jnp.where(table > 0.5, 0.0, blocked).astype(f32).transpose(0, 2, 1, 3).reshape(-1)

    scale = math.log2(math.e) / math.sqrt(HEAD_DIM)
    big = pl.BlockSpec((groups, rows, HEAD_DIM), lambda h, *_: (0, h, 0))
    small = pl.BlockSpec((rows, HEAD_DIM), lambda h, *_: (h, 0))

    def attend(g, bias):
        return pl.pallas_call(
            functools.partial(
                attend_kernel, slot_of_queries=g, groups=groups, layers=layers, scale=scale
            ),
            grid_spec=pltpu.PrefetchScalarGridSpec(
                num_scalar_prefetch=1,
                grid=(per_group,),
                in_specs=[small] + [big] * (2 * layers),
                out_specs=small,
                scratch_shapes=[pltpu.VMEM((devices, rows, rows), f32)],
            ),
            out_shape=jax.ShapeDtypeStruct((per_group * rows, HEAD_DIM), bf16),
            compiler_params=params,
            cost_estimate=pl.CostEstimate(
                flops=per_group * rows * devices * rows * HEAD_DIM * 4,
                bytes_accessed=per_group * devices * rows * HEAD_DIM * 5,
                transcendentals=per_group * rows * devices * rows,
            ),
            name=f"attend_{g}",
        )(bias, q_arrived[g], *keys, *values)

    outputs = [None] * groups
    for g in [*range(1, groups), 0]:
        own = attend(g, bias)
        outputs[g] = rotated(own, groups - g) if g else own
        if g:
            earlier = [outputs[g - 1]] if g > 1 else []
            own, bias, earlier = lax.optimization_barrier((own, bias, earlier))
            if g > 1:
                outputs[g - 1] = earlier[0]

    return pl.pallas_call(
        functools.partial(collect_kernel, per_group=per_group),
        out_shape=jax.ShapeDtypeStruct((rows, width), f32),
        in_specs=[SMEM] + [VMEM] * groups,
        out_specs=VMEM,
        compiler_params=params,
        name="collect",
    )(place_row, *outputs)


def normalized(inputs, gain_row, square_sum, full_width):
    return (inputs / jnp.sqrt(square_sum / full_width + epsilon)[:, None] * gain_row).astype(
        jnp.bfloat16
    )


def shards(q_in, k_in, v_in, q_gain, k_gain, frames, adjacent):
    tok_rows = q_in.shape[0]
    width_dev = q_in.shape[1]
    full_width = width_dev * lax.axis_size("tensor")
    q_sum, k_sum = lax.psum((jnp.sum(q_in * q_in, axis=1), jnp.sum(k_in * k_in, axis=1)), "tensor")
    q_norm = normalized(q_in, q_gain, q_sum, full_width)
    k_norm = normalized(k_in, k_gain, k_sum, full_width)
    blk_dev = tok_rows // BLOCK
    device = lax.axis_index("seq")
    first_block = device * blk_dev
    query_frames = lax.dynamic_slice_in_dim(frames, first_block, blk_dev, 0)
    score_scale = 1.0 / math.sqrt(HEAD_DIM)
    head_count = width_dev // HEAD_DIM
    q_three = q_norm.reshape(tok_rows, head_count, HEAD_DIM)

    def masked_scores(key_rows, key_start):
        key_block = key_start // BLOCK
        key_frames = lax.dynamic_slice_in_dim(frames, key_block, blk_dev, 0)
        adjacent_rows = lax.dynamic_slice_in_dim(adjacent, key_block, blk_dev, 1)
        frame_gap = jnp.abs(query_frames[:, None] - key_frames[None, :])
        allowed_here = (frame_gap == 0) | (frame_gap == 1) & (adjacent_rows == 1)
        key_three = key_rows.reshape(tok_rows, head_count, HEAD_DIM)
        raw_scores = (
            jnp.einsum("thd,uhd->htu", q_three, key_three, preferred_element_type=jnp.float32)
            * score_scale
        )
        tiled_scores = raw_scores.reshape(head_count, blk_dev, BLOCK, blk_dev, BLOCK)
        tiled_scores = jnp.where(allowed_here[None, :, None, :, None], tiled_scores, blocked)
        return tiled_scores.reshape(head_count, tok_rows, tok_rows)

    piece = lax.all_gather(k_norm, "seq", axis=0, tiled=True)
    shard_count = piece.shape[0] // tok_rows

    def one_shard(shard, current):
        key_rows = lax.dynamic_slice_in_dim(piece, shard * tok_rows, tok_rows, 0)
        return jnp.maximum(current, jnp.max(masked_scores(key_rows, shard * tok_rows), axis=2))

    row_max = lax.fori_loop(
        0, shard_count, one_shard, jnp.full((head_count, tok_rows), blocked, jnp.float32)
    )
    start_sums = (
        jnp.zeros((head_count, tok_rows), jnp.float32),
        jnp.zeros((tok_rows, head_count, HEAD_DIM), jnp.float32),
    )
    key_piece = lax.all_gather(k_norm, "seq", axis=0, tiled=True)
    value_piece = lax.all_gather(v_in, "seq", axis=0, tiled=True)
    shard_count = key_piece.shape[0] // tok_rows

    def one_shard(shard, current):
        totals, accumulated = current
        key_rows = lax.dynamic_slice_in_dim(key_piece, shard * tok_rows, tok_rows, 0)
        value_rows = lax.dynamic_slice_in_dim(value_piece, shard * tok_rows, tok_rows, 0).reshape(
            tok_rows, head_count, HEAD_DIM
        )
        weights = jnp.exp(masked_scores(key_rows, shard * tok_rows) - row_max[:, :, None])
        totals = totals + jnp.sum(weights, axis=2)
        accumulated = accumulated + jnp.einsum(
            "htu,uhd->thd",
            weights.astype(jnp.bfloat16),
            value_rows,
            preferred_element_type=jnp.float32,
        )
        return (totals, accumulated)

    totals, accumulated = lax.fori_loop(0, shard_count, one_shard, start_sums)
    return (accumulated / totals.T[:, :, None]).reshape(tok_rows, width_dev)


def groups_of(mesh, heads):
    layers = 4
    groups = mesh.shape["seq"] // layers
    fits = mesh.shape["seq"] % layers == 0 and heads % groups == 0 and heads >= 2 * groups
    return groups if fits else 1


def solution(mesh):
    def step(q_in, k_in, v_in, q_gain, k_gain, frames, adjacent):
        heads = q_in.shape[1] // mesh.shape["tensor"] // HEAD_DIM
        groups = groups_of(mesh, heads)
        body = shards if groups == 1 else functools.partial(exchanged, groups=groups)
        return jax.shard_map(
            body,
            mesh=mesh,
            in_specs=(
                P("seq", "tensor"),
                P("seq", "tensor"),
                P("seq", "tensor"),
                P("tensor"),
                P("tensor"),
                P(),
                P("seq", None),
            ),
            out_specs=P("seq", "tensor"),
            check_vma=False,
        )(q_in, k_in, v_in, q_gain, k_gain, frames, adjacent)

    return step
```

```python
import functools
import math

import jax
import jax.numpy as jnp
from jax import lax
from jax.experimental import pallas as pl
from jax.experimental.pallas import tpu as pltpu
from jax.sharding import PartitionSpec as P

HEAD_DIM = 128
BLOCK = 128
epsilon = 1e-06
blocked = -1e30
MASK_ROWS = 16
MIB = 1024 * 1024
VMEM = pl.BlockSpec(memory_space=pltpu.VMEM)
SMEM = pl.BlockSpec(memory_space=pltpu.SMEM)
ANY = pl.BlockSpec(memory_space=pl.ANY)


def column_of(place_ref, shift, head, groups, per_group):
    group = lax.rem(place_ref[0] + shift, groups)
    return pl.multiple_of((group * per_group + head) * HEAD_DIM, HEAD_DIM)


def value_kernel(place_ref, v_ref, *outs, per_group):
    groups = len(outs)
    rows = v_ref.shape[0]
    for shift, out in enumerate(outs):
        for head in range(per_group):
            column = column_of(place_ref, shift, head, groups, per_group)
            out[head * rows : (head + 1) * rows, :] = v_ref[:, pl.ds(column, HEAD_DIM)]


def square_sums_kernel(q_ref, k_ref, out_ref):
    q, k = q_ref[...], k_ref[...]
    out_ref[:, 0:1] = jnp.sum(q * q, axis=1, keepdims=True)
    out_ref[:, 1:2] = jnp.sum(k * k, axis=1, keepdims=True)


def normed_columns(x_ref, inverse, gain_ref, column):
    here = pl.ds(column, HEAD_DIM)
    return (x_ref[:, here] * inverse * gain_ref[:, here]).astype(jnp.bfloat16)


def norm_kernel(
    place_ref, sums_ref, q_ref, k_ref, q_gain_ref, k_gain_ref, mask_ref, *outs, per_group, full_width
):
    groups = len(outs) // 2
    rows = k_ref.shape[0]
    inverse = 1.0 / jnp.sqrt(sums_ref[...] / full_width + epsilon)
    for shift in range(groups):
        k_out, q_out = outs[shift], outs[groups + shift]
        for head in range(per_group):
            column = column_of(place_ref, shift, head, groups, per_group)
            q_out[head * rows : (head + 1) * rows, :] = normed_columns(
                q_ref, inverse[:, 0:1], q_gain_ref, column
            )
            k = normed_columns(k_ref, inverse[:, 1:2], k_gain_ref, column)
            for b in range(rows // BLOCK):
                low = head * rows + b * HEAD_DIM
                k_out[low : low + HEAD_DIM, :] = k[b * BLOCK : (b + 1) * BLOCK].T
        k_out[per_group * rows :, :] = mask_ref[...]


def attend_kernel(bias_ref, q_ref, *refs, query_slot, groups, layers, heads, scale):
    k_refs, v_refs = refs[:layers], refs[layers : 2 * layers]
    out, scores = refs[-2:]
    rows = out.shape[0] // len(heads)
    blk = rows // BLOCK
    slots = groups * layers
    lowest = jnp.full((rows, BLOCK), blocked, jnp.float32)
    ones = jnp.ones((rows, HEAD_DIM), jnp.bfloat16)

    def score(head, slot, top, q):
        keys = k_refs[slot // groups][slot % groups, head * rows : (head + 1) * rows, :]
        wide = jnp.concatenate(
            [keys[b * HEAD_DIM : (b + 1) * HEAD_DIM] for b in range(blk)], axis=1
        )
        products = jnp.dot(q, wide, preferred_element_type=jnp.float32)
        first = (query_slot * slots + slot) * blk
        for b in range(blk):
            columns = slice(b * BLOCK, (b + 1) * BLOCK)
            block = jnp.concatenate(
                [
                    products[a * BLOCK : (a + 1) * BLOCK, columns] + bias_ref[(first + a) * blk + b]
                    for a in range(blk)
                ],
                axis=0,
            )
            scores[head % 2, slot, :, columns] = block
            top = jnp.maximum(top, block)
        return top

    def weigh(head, slot, row_max, mixed):
        weights = jnp.exp2((scores[head % 2, slot] - row_max) * scale).astype(jnp.bfloat16)
        values = v_refs[slot // groups][slot % groups, head * rows : (head + 1) * rows, :]
        return mixed + jnp.dot(
            weights, jnp.concatenate([values, ones], axis=1), preferred_element_type=jnp.float32
        )

    top, q = lowest, q_ref[heads[0] * rows : (heads[0] + 1) * rows, :]
    for slot in range(slots):
        top = score(heads[0], slot, top, q)
    for head in heads:
        row_max = jnp.max(top, axis=1, keepdims=True)
        mixed, top = jnp.zeros((rows, 2 * HEAD_DIM), jnp.float32), lowest
        if head + 1 in heads:
            q = q_ref[(head + 1) * rows : (head + 2) * rows, :]
        for slot in range(slots):
            if head + 1 in heads:
                top = score(head + 1, slot, top, q)
            mixed = weigh(head, slot, row_max, mixed)
        low = (head - heads[0]) * rows
        out[low : low + rows, :] = (
            mixed[:, :HEAD_DIM] / mixed[:, HEAD_DIM : HEAD_DIM + 1]
        ).astype(jnp.bfloat16)


def collect_kernel(place_ref, *refs, groups, per_group):
    out = refs[-1]
    rows = out.shape[0]
    first = refs[0].shape[0] // rows
    for shift in range(groups):
        for head in range(per_group):
            if shift:
                ref, low = refs[shift + 1], head * rows
            elif head < first:
                ref, low = refs[0], head * rows
            else:
                ref, low = refs[1], (head - first) * rows
            column = column_of(place_ref, shift, head, groups, per_group)
            out[:, pl.ds(column, HEAD_DIM)] = ref[low : low + rows, :].astype(jnp.float32)


def exchanged(q_in, k_in, v_in, q_gain, k_gain, frames, adjacent, *, groups):
    rows, width = q_in.shape
    devices = lax.axis_size("seq")
    tensors = lax.axis_size("tensor")
    layers = devices // groups
    blk = rows // BLOCK
    blocks = devices * blk
    per_group = width // HEAD_DIM // groups
    me = lax.axis_index("seq")
    place, spot = me // layers, lax.rem(me, layers)
    place_row = place.reshape(1).astype(jnp.int32)
    f32, bf16 = jnp.float32, jnp.bfloat16
    params = pltpu.CompilerParams(vmem_limit_bytes=20 * MIB)
    def rotated(x, shift):
        pairs = [
            (z * layers + r, (z + shift) % groups * layers + r)
            for z in range(groups)
            for r in range(layers)
        ]
        return lax.ppermute(x, "seq", pairs)

    def exchange(pieces, after=None):
        arrived = [pieces[0]]
        for s in range(1, groups):
            piece = pieces[s]
            if after is not None:
                piece, after[s] = lax.optimization_barrier((piece, after[s]))
            arrived.append(rotated(piece, s))
        return arrived

    def swapped(x, bit):
        return lax.ppermute(x, "seq", [(i, i ^ bit) for i in range(devices)])

    own_frames = lax.dynamic_slice_in_dim(frames, me * blk, blk, 0)
    gap = jnp.abs(own_frames[:, None] - frames[None, :])
    allowed = ((gap == 0) | (gap == 1) & (adjacent == 1)).astype(bf16)
    mask_rows = jnp.pad(allowed, ((0, MASK_ROWS - blk), (0, BLOCK - blocks)))

    v_pieces = pl.pallas_call(
        functools.partial(value_kernel, per_group=per_group),
        out_shape=[jax.ShapeDtypeStruct((per_group * rows, HEAD_DIM), bf16)] * groups,
        in_specs=[SMEM, VMEM],
        out_specs=[VMEM] * groups,
        compiler_params=params,
        name="value_pieces",
    )(place_row, v_in)
    q_in, k_in, v_pieces = lax.optimization_barrier((q_in, k_in, v_pieces))
    sums = pl.pallas_call(
        square_sums_kernel,
        out_shape=jax.ShapeDtypeStruct((rows, 2), f32),
        in_specs=[VMEM, VMEM],
        out_specs=VMEM,
        compiler_params=params,
        name="square_sums",
    )(q_in, k_in)
    v_arrived = exchange(v_pieces)
    sums = lax.psum(sums, "tensor")

    piece = jax.ShapeDtypeStruct((per_group * rows, HEAD_DIM), bf16)
    masked_piece = jax.ShapeDtypeStruct((per_group * rows + MASK_ROWS, HEAD_DIM), bf16)
    pieces = pl.pallas_call(
        functools.partial(
            norm_kernel, per_group=per_group, full_width=float(width * tensors)
        ),
        out_shape=[masked_piece] * groups + [piece] * groups,
        in_specs=[SMEM] + [VMEM] * 6,
        out_specs=[VMEM] * (2 * groups),
        compiler_params=params,
        name="norm_pieces",
    )(place_row, sums, q_in, k_in, q_gain.reshape(1, width), k_gain.reshape(1, width), mask_rows)
    k_arrived = exchange(pieces[:groups], v_arrived)
    v_stack = jnp.stack(v_arrived)
    q_arrived = exchange(pieces[groups:], k_arrived)

    low = per_group * rows
    known = jnp.stack([x[low : low + blk, :blocks] for x in k_arrived]).astype(f32)
    z_order = lax.rem(place - jnp.arange(groups) + groups, groups)
    layer_order = jnp.bitwise_xor(spot, jnp.arange(layers))
    key_blocks = (
        (z_order[None, :, None] * layers + layer_order[:, None, None]) * blk
        + jnp.arange(blk)[None, None, :]
    ).reshape(-1)
    key_hot = (key_blocks[:, None] == jnp.arange(blocks)[None, :]).astype(f32)
    table = jnp.einsum("gab,kb->gak", known, key_hot).reshape(groups, blk, devices, blk)
    bias = jnp.where(table > 0.5, 0.0, blocked).astype(f32).transpose(0, 2, 1, 3).reshape(-1)

    def spread(parts, bit):
        return parts | {have ^ bit: swapped(part, bit) for have, part in parts.items()}

    bits = [1 << i for i in reversed(range(layers.bit_length() - 1))]
    values, keys = {0: v_stack}, {}
    for bit in bits:
        values = spread(values, bit)
        if bit == bits[0]:
            k_arrived, values = lax.optimization_barrier((k_arrived, values))
            keys = {0: jnp.stack([x[: per_group * rows] for x in k_arrived])}
    for bit in bits:
        keys = spread(keys, bit)
        if bit == bits[0]:
            q_arrived, keys, bias = lax.optimization_barrier((q_arrived, keys, bias))
    values = [values[i] for i in range(layers)]
    keys = [keys[i] for i in range(layers)]

    scale = math.log2(math.e) / math.sqrt(HEAD_DIM)
    def attend(g, heads, bias):
        return pl.pallas_call(
            functools.partial(
                attend_kernel,
                query_slot=g,
                groups=groups,
                layers=layers,
                heads=heads,
                scale=scale,
            ),
            in_specs=[SMEM] + [VMEM] * (1 + 2 * layers),
            out_specs=VMEM,
            scratch_shapes=[pltpu.VMEM((2, devices, rows, rows), f32)],
            out_shape=jax.ShapeDtypeStruct((len(heads) * rows, HEAD_DIM), bf16),
            compiler_params=params,
            name=f"attend_{g}_{heads[0]}",
        )(bias, q_arrived[g], *keys, *values)

    order = sorted(range(1, groups), key=lambda s: abs(2 * s - groups))
    outputs, last = [None] * groups, None
    for g in order:
        own = attend(g, range(per_group), bias)
        outputs[g] = rotated(own, groups - g)
        own, bias = lax.optimization_barrier((own, bias))
    parts = []
    for i, heads in enumerate((range(per_group - 2), range(per_group - 2, per_group))):
        if i < len(order) - 1:
            outputs[order[i]], bias = lax.optimization_barrier((outputs[order[i]], bias))
        parts.append(attend(0, heads, bias))
        parts[-1], bias = lax.optimization_barrier((parts[-1], bias))

    return pl.pallas_call(
        functools.partial(collect_kernel, groups=groups, per_group=per_group),
        out_shape=jax.ShapeDtypeStruct((rows, width), f32),
        in_specs=[SMEM] + [VMEM] * (groups + 1),
        out_specs=VMEM,
        compiler_params=params,
        name="collect",
    )(place_row, *parts, *outputs[1:])


def normalized(inputs, gain_row, square_sum, full_width):
    return (inputs / jnp.sqrt(square_sum / full_width + epsilon)[:, None] * gain_row).astype(
        jnp.bfloat16
    )


def shards(q_in, k_in, v_in, q_gain, k_gain, frames, adjacent):
    tok_rows = q_in.shape[0]
    width_dev = q_in.shape[1]
    full_width = width_dev * lax.axis_size("tensor")
    q_sum, k_sum = lax.psum((jnp.sum(q_in * q_in, axis=1), jnp.sum(k_in * k_in, axis=1)), "tensor")
    q_norm = normalized(q_in, q_gain, q_sum, full_width)
    k_norm = normalized(k_in, k_gain, k_sum, full_width)
    blk_dev = tok_rows // BLOCK
    device = lax.axis_index("seq")
    first_block = device * blk_dev
    query_frames = lax.dynamic_slice_in_dim(frames, first_block, blk_dev, 0)
    score_scale = 1.0 / math.sqrt(HEAD_DIM)
    head_count = width_dev // HEAD_DIM
    q_three = q_norm.reshape(tok_rows, head_count, HEAD_DIM)

    def masked_scores(key_rows, key_start):
        key_block = key_start // BLOCK
        key_frames = lax.dynamic_slice_in_dim(frames, key_block, blk_dev, 0)
        adjacent_rows = lax.dynamic_slice_in_dim(adjacent, key_block, blk_dev, 1)
        frame_gap = jnp.abs(query_frames[:, None] - key_frames[None, :])
        allowed_here = (frame_gap == 0) | (frame_gap == 1) & (adjacent_rows == 1)
        key_three = key_rows.reshape(tok_rows, head_count, HEAD_DIM)
        raw_scores = (
            jnp.einsum("thd,uhd->htu", q_three, key_three, preferred_element_type=jnp.float32)
            * score_scale
        )
        tiled_scores = raw_scores.reshape(head_count, blk_dev, BLOCK, blk_dev, BLOCK)
        tiled_scores = jnp.where(allowed_here[None, :, None, :, None], tiled_scores, blocked)
        return tiled_scores.reshape(head_count, tok_rows, tok_rows)

    piece = lax.all_gather(k_norm, "seq", axis=0, tiled=True)
    shard_count = piece.shape[0] // tok_rows

    def one_shard(shard, current):
        key_rows = lax.dynamic_slice_in_dim(piece, shard * tok_rows, tok_rows, 0)
        return jnp.maximum(current, jnp.max(masked_scores(key_rows, shard * tok_rows), axis=2))

    row_max = lax.fori_loop(
        0, shard_count, one_shard, jnp.full((head_count, tok_rows), blocked, jnp.float32)
    )
    start_sums = (
        jnp.zeros((head_count, tok_rows), jnp.float32),
        jnp.zeros((tok_rows, head_count, HEAD_DIM), jnp.float32),
    )
    key_piece = lax.all_gather(k_norm, "seq", axis=0, tiled=True)
    value_piece = lax.all_gather(v_in, "seq", axis=0, tiled=True)
    shard_count = key_piece.shape[0] // tok_rows

    def one_shard(shard, current):
        totals, accumulated = current
        key_rows = lax.dynamic_slice_in_dim(key_piece, shard * tok_rows, tok_rows, 0)
        value_rows = lax.dynamic_slice_in_dim(value_piece, shard * tok_rows, tok_rows, 0).reshape(
            tok_rows, head_count, HEAD_DIM
        )
        weights = jnp.exp(masked_scores(key_rows, shard * tok_rows) - row_max[:, :, None])
        totals = totals + jnp.sum(weights, axis=2)
        accumulated = accumulated + jnp.einsum(
            "htu,uhd->thd",
            weights.astype(jnp.bfloat16),
            value_rows,
            preferred_element_type=jnp.float32,
        )
        return (totals, accumulated)

    totals, accumulated = lax.fori_loop(0, shard_count, one_shard, start_sums)
    return (accumulated / totals.T[:, :, None]).reshape(tok_rows, width_dev)


def groups_of(mesh, heads):
    layers = 4
    groups = mesh.shape["seq"] // layers
    fits = mesh.shape["seq"] % layers == 0 and heads % groups == 0 and heads >= 2 * groups
    return groups if fits else 1


def solution(mesh):
    def step(q_in, k_in, v_in, q_gain, k_gain, frames, adjacent):
        heads = q_in.shape[1] // mesh.shape["tensor"] // HEAD_DIM
        groups = groups_of(mesh, heads)
        body = shards if groups == 1 else functools.partial(exchanged, groups=groups)
        return jax.shard_map(
            body,
            mesh=mesh,
            in_specs=(
                P("seq", "tensor"),
                P("seq", "tensor"),
                P("seq", "tensor"),
                P("tensor"),
                P("tensor"),
                P(),
                P("seq", None),
            ),
            out_specs=P("seq", "tensor"),
            check_vma=False,
        )(q_in, k_in, v_in, q_gain, k_gain, frames, adjacent)

    return step
```

```python
import functools
import math

import jax
import jax.numpy as jnp
from jax import lax
from jax.experimental import pallas as pl
from jax.experimental.pallas import tpu as pltpu
from jax.sharding import PartitionSpec as P

HEAD_DIM = 128
BLOCK = 128
epsilon = 1e-06
blocked = -1e30
MASK_ROWS = 16
MIB = 1024 * 1024
VMEM = pl.BlockSpec(memory_space=pltpu.VMEM)
SMEM = pl.BlockSpec(memory_space=pltpu.SMEM)
ANY = pl.BlockSpec(memory_space=pl.ANY)


def column_of(place_ref, shift, head, groups, per_group):
    group = lax.rem(place_ref[0] + shift, groups)
    return pl.multiple_of((group * per_group + head) * HEAD_DIM, HEAD_DIM)


def value_kernel(place_ref, v_ref, *outs, per_group):
    groups = len(outs)
    rows = v_ref.shape[0]
    for shift, out in enumerate(outs):
        for head in range(per_group):
            column = column_of(place_ref, shift, head, groups, per_group)
            out[head * rows : (head + 1) * rows, :] = v_ref[:, pl.ds(column, HEAD_DIM)]


def square_sums_kernel(q_ref, k_ref, out_ref):
    q, k = q_ref[...], k_ref[...]
    out_ref[:, 0:1] = jnp.sum(q * q, axis=1, keepdims=True)
    out_ref[:, 1:2] = jnp.sum(k * k, axis=1, keepdims=True)


def normed_columns(x_ref, inverse, gain_ref, column):
    here = pl.ds(column, HEAD_DIM)
    return (x_ref[:, here] * inverse * gain_ref[:, here]).astype(jnp.bfloat16)


def norm_kernel(
    place_ref, sums_ref, q_ref, k_ref, q_gain_ref, k_gain_ref, mask_ref, *outs, per_group, full_width
):
    groups = len(outs) // 2
    rows = k_ref.shape[0]
    inverse = 1.0 / jnp.sqrt(sums_ref[...] / full_width + epsilon)
    for shift in range(groups):
        k_out, q_out = outs[shift], outs[groups + shift]
        for head in range(per_group):
            column = column_of(place_ref, shift, head, groups, per_group)
            q_out[head * rows : (head + 1) * rows, :] = normed_columns(
                q_ref, inverse[:, 0:1], q_gain_ref, column
            )
            k = normed_columns(k_ref, inverse[:, 1:2], k_gain_ref, column)
            for b in range(rows // BLOCK):
                low = head * rows + b * HEAD_DIM
                k_out[low : low + HEAD_DIM, :] = k[b * BLOCK : (b + 1) * BLOCK].T
        k_out[per_group * rows :, :] = mask_ref[...]


def attend_kernel(bias_ref, *refs, query_slots, groups, layers, heads, scale):
    count = len(query_slots)
    q_refs, refs = refs[:count], refs[count:]
    k_refs, v_refs = refs[:layers], refs[layers : 2 * layers]
    outs, scores = refs[2 * layers : -1], refs[-1]
    rows = outs[0].shape[0] // heads
    blk = rows // BLOCK
    slots = groups * layers
    lowest = jnp.full((rows, BLOCK), blocked, jnp.float32)
    ones = jnp.ones((rows, HEAD_DIM), jnp.bfloat16)
    units = [(i, head) for head in range(heads) for i in range(count)]

    def score(u, slot, top, q):
        i, head = units[u]
        keys = k_refs[slot // groups][slot % groups, head * rows : (head + 1) * rows, :]
        wide = jnp.concatenate(
            [keys[b * HEAD_DIM : (b + 1) * HEAD_DIM] for b in range(blk)], axis=1
        )
        products = jnp.dot(q, wide, preferred_element_type=jnp.float32)
        first = (query_slots[i] * slots + slot) * blk
        for b in range(blk):
            columns = slice(b * BLOCK, (b + 1) * BLOCK)
            block = jnp.concatenate(
                [
                    products[a * BLOCK : (a + 1) * BLOCK, columns] + bias_ref[(first + a) * blk + b]
                    for a in range(blk)
                ],
                axis=0,
            )
            scores[u % 2, slot, :, columns] = block
            top = jnp.maximum(top, block)
        return top

    def weigh(u, slot, row_max, mixed):
        head = units[u][1]
        weights = jnp.exp2((scores[u % 2, slot] - row_max) * scale).astype(jnp.bfloat16)
        values = v_refs[slot // groups][slot % groups, head * rows : (head + 1) * rows, :]
        return mixed + jnp.dot(
            weights, jnp.concatenate([values, ones], axis=1), preferred_element_type=jnp.float32
        )

    def queries(u):
        i, head = units[u]
        return q_refs[i][head * rows : (head + 1) * rows, :]

    top, q = lowest, queries(0)
    for slot in range(slots):
        top = score(0, slot, top, q)
    for u, (i, head) in enumerate(units):
        row_max = jnp.max(top, axis=1, keepdims=True)
        mixed, top = jnp.zeros((rows, 2 * HEAD_DIM), jnp.float32), lowest
        if u + 1 < len(units):
            q = queries(u + 1)
        for slot in range(slots):
            if u + 1 < len(units):
                top = score(u + 1, slot, top, q)
            mixed = weigh(u, slot, row_max, mixed)
        outs[i][head * rows : (head + 1) * rows, :] = (
            mixed[:, :HEAD_DIM] / mixed[:, HEAD_DIM : HEAD_DIM + 1]
        ).astype(jnp.bfloat16)


def collect_kernel(place_ref, *refs, per_group):
    out = refs[-1]
    groups = len(refs) - 1
    rows = out.shape[0]
    for shift in range(groups):
        for head in range(per_group):
            column = column_of(place_ref, shift, head, groups, per_group)
            piece = refs[shift][head * rows : (head + 1) * rows, :]
            out[:, pl.ds(column, HEAD_DIM)] = piece.astype(jnp.float32)


def exchanged(q_in, k_in, v_in, q_gain, k_gain, frames, adjacent, *, groups):
    rows, width = q_in.shape
    devices = lax.axis_size("seq")
    tensors = lax.axis_size("tensor")
    layers = devices // groups
    blk = rows // BLOCK
    blocks = devices * blk
    per_group = width // HEAD_DIM // groups
    me = lax.axis_index("seq")
    place, spot = me // layers, lax.rem(me, layers)
    place_row = place.reshape(1).astype(jnp.int32)
    f32, bf16 = jnp.float32, jnp.bfloat16
    params = pltpu.CompilerParams(vmem_limit_bytes=20 * MIB)
    def rotated(x, shift):
        pairs = [
            (z * layers + r, (z + shift) % groups * layers + r)
            for z in range(groups)
            for r in range(layers)
        ]
        return lax.ppermute(x, "seq", pairs)

    def exchange(pieces, after=None):
        shifts = range(1, groups)
        arrived = list(pieces)
        for s in shifts:
            if after is not None:
                arrived[s], after[s] = lax.optimization_barrier((arrived[s], after[s]))
            arrived[s] = rotated(arrived[s], s)
        return arrived

    def swapped(x, bit):
        return lax.ppermute(x, "seq", [(i, i ^ bit) for i in range(devices)])

    own_frames = lax.dynamic_slice_in_dim(frames, me * blk, blk, 0)
    gap = jnp.abs(own_frames[:, None] - frames[None, :])
    allowed = ((gap == 0) | (gap == 1) & (adjacent == 1)).astype(bf16)
    mask_rows = jnp.pad(allowed, ((0, MASK_ROWS - blk), (0, BLOCK - blocks)))

    v_pieces = pl.pallas_call(
        functools.partial(value_kernel, per_group=per_group),
        out_shape=[jax.ShapeDtypeStruct((per_group * rows, HEAD_DIM), bf16)] * groups,
        in_specs=[SMEM, VMEM],
        out_specs=[VMEM] * groups,
        compiler_params=params,
        name="value_pieces",
    )(place_row, v_in)
    q_in, k_in, v_pieces = lax.optimization_barrier((q_in, k_in, v_pieces))
    sums = pl.pallas_call(
        square_sums_kernel,
        out_shape=jax.ShapeDtypeStruct((rows, 2), f32),
        in_specs=[VMEM, VMEM],
        out_specs=VMEM,
        compiler_params=params,
        name="square_sums",
    )(q_in, k_in)
    v_arrived = exchange(v_pieces)
    sums = lax.psum(sums, "tensor")

    piece = jax.ShapeDtypeStruct((per_group * rows, HEAD_DIM), bf16)
    masked_piece = jax.ShapeDtypeStruct((per_group * rows + MASK_ROWS, HEAD_DIM), bf16)
    pieces = pl.pallas_call(
        functools.partial(
            norm_kernel, per_group=per_group, full_width=float(width * tensors)
        ),
        out_shape=[masked_piece] * groups + [piece] * groups,
        in_specs=[SMEM] + [VMEM] * 6,
        out_specs=[VMEM] * (2 * groups),
        compiler_params=params,
        name="norm_pieces",
    )(place_row, sums, q_in, k_in, q_gain.reshape(1, width), k_gain.reshape(1, width), mask_rows)
    k_arrived = exchange(pieces[:groups], v_arrived)
    v_stack = jnp.stack(v_arrived)
    q_arrived = exchange(pieces[groups:], k_arrived)

    low = per_group * rows
    known = jnp.stack([x[low : low + blk, :blocks] for x in k_arrived]).astype(f32)
    z_order = lax.rem(place - jnp.arange(groups) + groups, groups)
    layer_order = jnp.bitwise_xor(spot, jnp.arange(layers))
    key_blocks = (
        (z_order[None, :, None] * layers + layer_order[:, None, None]) * blk
        + jnp.arange(blk)[None, None, :]
    ).reshape(-1)
    key_hot = (key_blocks[:, None] == jnp.arange(blocks)[None, :]).astype(f32)
    table = jnp.einsum("gab,kb->gak", known, key_hot).reshape(groups, blk, devices, blk)
    bias = jnp.where(table > 0.5, 0.0, blocked).astype(f32).transpose(0, 2, 1, 3).reshape(-1)

    def spread(parts, bit):
        return parts | {have ^ bit: swapped(part, bit) for have, part in parts.items()}

    bits = [1 << i for i in reversed(range(layers.bit_length() - 1))]
    values, keys = {0: v_stack}, {}
    for bit in bits:
        values = spread(values, bit)
        if bit == bits[0]:
            k_arrived, values = lax.optimization_barrier((k_arrived, values))
            keys = {0: jnp.stack([x[: per_group * rows] for x in k_arrived])}
    for bit in bits:
        keys = spread(keys, bit)
        if bit == bits[0]:
            q_arrived, keys, bias = lax.optimization_barrier((q_arrived, keys, bias))
    values = [values[i] for i in range(layers)]
    keys = [keys[i] for i in range(layers)]

    scale = math.log2(math.e) / math.sqrt(HEAD_DIM)
    def attend(query_slots, bias):
        return pl.pallas_call(
            functools.partial(
                attend_kernel,
                query_slots=query_slots,
                groups=groups,
                layers=layers,
                heads=per_group,
                scale=scale,
            ),
            in_specs=[SMEM] + [VMEM] * (len(query_slots) + 2 * layers),
            out_specs=[VMEM] * len(query_slots),
            scratch_shapes=[pltpu.VMEM((2, devices, rows, rows), f32)],
            out_shape=[jax.ShapeDtypeStruct((per_group * rows, HEAD_DIM), bf16)] * len(query_slots),
            compiler_params=params,
            name="attend_" + "_".join(str(g) for g in query_slots),
        )(bias, *[q_arrived[g] for g in query_slots], *keys, *values)

    outputs = [None] * groups
    far = groups // 2
    near = tuple(g for g in range(1, groups) if g != far)
    for query_slots in ((far,), near, (0,)):
        if query_slots == (0,):
            outputs[far], bias = lax.optimization_barrier((outputs[far], bias))
        own = attend(query_slots, bias)
        own, bias = lax.optimization_barrier((own, bias))
        for g, x in zip(query_slots, own):
            outputs[g] = rotated(x, groups - g) if g else x

    return pl.pallas_call(
        functools.partial(collect_kernel, per_group=per_group),
        out_shape=jax.ShapeDtypeStruct((rows, width), f32),
        in_specs=[SMEM] + [VMEM] * groups,
        out_specs=VMEM,
        compiler_params=params,
        name="collect",
    )(place_row, *outputs)


def normalized(inputs, gain_row, square_sum, full_width):
    return (inputs / jnp.sqrt(square_sum / full_width + epsilon)[:, None] * gain_row).astype(
        jnp.bfloat16
    )


def shards(q_in, k_in, v_in, q_gain, k_gain, frames, adjacent):
    tok_rows = q_in.shape[0]
    width_dev = q_in.shape[1]
    full_width = width_dev * lax.axis_size("tensor")
    q_sum, k_sum = lax.psum((jnp.sum(q_in * q_in, axis=1), jnp.sum(k_in * k_in, axis=1)), "tensor")
    q_norm = normalized(q_in, q_gain, q_sum, full_width)
    k_norm = normalized(k_in, k_gain, k_sum, full_width)
    blk_dev = tok_rows // BLOCK
    device = lax.axis_index("seq")
    first_block = device * blk_dev
    query_frames = lax.dynamic_slice_in_dim(frames, first_block, blk_dev, 0)
    score_scale = 1.0 / math.sqrt(HEAD_DIM)
    head_count = width_dev // HEAD_DIM
    q_three = q_norm.reshape(tok_rows, head_count, HEAD_DIM)

    def masked_scores(key_rows, key_start):
        key_block = key_start // BLOCK
        key_frames = lax.dynamic_slice_in_dim(frames, key_block, blk_dev, 0)
        adjacent_rows = lax.dynamic_slice_in_dim(adjacent, key_block, blk_dev, 1)
        frame_gap = jnp.abs(query_frames[:, None] - key_frames[None, :])
        allowed_here = (frame_gap == 0) | (frame_gap == 1) & (adjacent_rows == 1)
        key_three = key_rows.reshape(tok_rows, head_count, HEAD_DIM)
        raw_scores = (
            jnp.einsum("thd,uhd->htu", q_three, key_three, preferred_element_type=jnp.float32)
            * score_scale
        )
        tiled_scores = raw_scores.reshape(head_count, blk_dev, BLOCK, blk_dev, BLOCK)
        tiled_scores = jnp.where(allowed_here[None, :, None, :, None], tiled_scores, blocked)
        return tiled_scores.reshape(head_count, tok_rows, tok_rows)

    piece = lax.all_gather(k_norm, "seq", axis=0, tiled=True)
    shard_count = piece.shape[0] // tok_rows

    def one_shard(shard, current):
        key_rows = lax.dynamic_slice_in_dim(piece, shard * tok_rows, tok_rows, 0)
        return jnp.maximum(current, jnp.max(masked_scores(key_rows, shard * tok_rows), axis=2))

    row_max = lax.fori_loop(
        0, shard_count, one_shard, jnp.full((head_count, tok_rows), blocked, jnp.float32)
    )
    start_sums = (
        jnp.zeros((head_count, tok_rows), jnp.float32),
        jnp.zeros((tok_rows, head_count, HEAD_DIM), jnp.float32),
    )
    key_piece = lax.all_gather(k_norm, "seq", axis=0, tiled=True)
    value_piece = lax.all_gather(v_in, "seq", axis=0, tiled=True)
    shard_count = key_piece.shape[0] // tok_rows

    def one_shard(shard, current):
        totals, accumulated = current
        key_rows = lax.dynamic_slice_in_dim(key_piece, shard * tok_rows, tok_rows, 0)
        value_rows = lax.dynamic_slice_in_dim(value_piece, shard * tok_rows, tok_rows, 0).reshape(
            tok_rows, head_count, HEAD_DIM
        )
        weights = jnp.exp(masked_scores(key_rows, shard * tok_rows) - row_max[:, :, None])
        totals = totals + jnp.sum(weights, axis=2)
        accumulated = accumulated + jnp.einsum(
            "htu,uhd->thd",
            weights.astype(jnp.bfloat16),
            value_rows,
            preferred_element_type=jnp.float32,
        )
        return (totals, accumulated)

    totals, accumulated = lax.fori_loop(0, shard_count, one_shard, start_sums)
    return (accumulated / totals.T[:, :, None]).reshape(tok_rows, width_dev)


def groups_of(mesh, heads):
    layers = 4
    groups = mesh.shape["seq"] // layers
    fits = groups & (groups - 1) == 0 and mesh.shape["seq"] == groups * layers
    fits = fits and heads % groups == 0 and heads >= 3 * groups
    return groups if fits else 1


def solution(mesh):
    def step(q_in, k_in, v_in, q_gain, k_gain, frames, adjacent):
        heads = q_in.shape[1] // mesh.shape["tensor"] // HEAD_DIM
        groups = groups_of(mesh, heads)
        body = shards if groups == 1 else functools.partial(exchanged, groups=groups)
        return jax.shard_map(
            body,
            mesh=mesh,
            in_specs=(
                P("seq", "tensor"),
                P("seq", "tensor"),
                P("seq", "tensor"),
                P("tensor"),
                P("tensor"),
                P(),
                P("seq", None),
            ),
            out_specs=P("seq", "tensor"),
            check_vma=False,
        )(q_in, k_in, v_in, q_gain, k_gain, frames, adjacent)

    return step
```

```python
import functools
import math

import jax
import jax.numpy as jnp
from jax import lax
from jax.experimental import pallas as pl
from jax.experimental.pallas import tpu as pltpu
from jax.sharding import PartitionSpec as P

HEAD_DIM = 128
BLOCK = 128
epsilon = 1e-06
blocked = -1e30
MASK_ROWS = 16
MIB = 1024 * 1024
VMEM = pl.BlockSpec(memory_space=pltpu.VMEM)
SMEM = pl.BlockSpec(memory_space=pltpu.SMEM)
ANY = pl.BlockSpec(memory_space=pl.ANY)


def column_of(place_ref, shift, head, groups, per_group):
    group = lax.rem(place_ref[0] + shift, groups)
    return pl.multiple_of((group * per_group + head) * HEAD_DIM, HEAD_DIM)


def value_kernel(place_ref, v_ref, *outs, per_group):
    groups = len(outs)
    rows = v_ref.shape[0]
    for shift, out in enumerate(outs):
        for head in range(per_group):
            column = column_of(place_ref, shift, head, groups, per_group)
            out[head * rows : (head + 1) * rows, :] = v_ref[:, pl.ds(column, HEAD_DIM)]


def square_sums_kernel(q_ref, k_ref, out_ref):
    q, k = q_ref[...], k_ref[...]
    out_ref[:, 0:1] = jnp.sum(q * q, axis=1, keepdims=True)
    out_ref[:, 1:2] = jnp.sum(k * k, axis=1, keepdims=True)


def normed_columns(x_ref, inverse, gain_ref, column):
    here = pl.ds(column, HEAD_DIM)
    return (x_ref[:, here] * inverse * gain_ref[:, here]).astype(jnp.bfloat16)


def norm_kernel(
    place_ref, sums_ref, q_ref, k_ref, q_gain_ref, k_gain_ref, mask_ref, *outs, per_group, full_width
):
    groups = len(outs) // 2
    rows = k_ref.shape[0]
    inverse = 1.0 / jnp.sqrt(sums_ref[...] / full_width + epsilon)
    for shift in range(groups):
        k_out, q_out = outs[shift], outs[groups + shift]
        for head in range(per_group):
            column = column_of(place_ref, shift, head, groups, per_group)
            q_out[head * rows : (head + 1) * rows, :] = normed_columns(
                q_ref, inverse[:, 0:1], q_gain_ref, column
            )
            k = normed_columns(k_ref, inverse[:, 1:2], k_gain_ref, column)
            for b in range(rows // BLOCK):
                low = head * rows + b * HEAD_DIM
                k_out[low : low + HEAD_DIM, :] = k[b * BLOCK : (b + 1) * BLOCK].T
        k_out[per_group * rows :, :] = mask_ref[...]


def attend_kernel(bias_ref, *refs, query_slots, groups, layers, heads, scale):
    count = len(query_slots)
    q_refs, refs = refs[:count], refs[count:]
    k_refs, v_refs = refs[:layers], refs[layers : 2 * layers]
    outs, scores = refs[2 * layers : -1], refs[-1]
    rows = outs[0].shape[0] // heads
    blk = rows // BLOCK
    slots = groups * layers
    lowest = jnp.full((rows, BLOCK), blocked, jnp.float32)
    ones = jnp.ones((rows, HEAD_DIM), jnp.bfloat16)
    units = [(i, head) for head in range(heads) for i in range(count)]

    def score(u, slot, top, q):
        i, head = units[u]
        keys = k_refs[slot // groups][slot % groups, head * rows : (head + 1) * rows, :]
        wide = jnp.concatenate(
            [keys[b * HEAD_DIM : (b + 1) * HEAD_DIM] for b in range(blk)], axis=1
        )
        products = jnp.dot(q, wide, preferred_element_type=jnp.float32)
        first = (query_slots[i] * slots + slot) * blk
        for b in range(blk):
            columns = slice(b * BLOCK, (b + 1) * BLOCK)
            block = jnp.concatenate(
                [
                    products[a * BLOCK : (a + 1) * BLOCK, columns] + bias_ref[(first + a) * blk + b]
                    for a in range(blk)
                ],
                axis=0,
            )
            scores[u % 2, slot, :, columns] = block
            top = jnp.maximum(top, block)
        return top

    def weigh(u, slot, row_max, mixed):
        head = units[u][1]
        weights = jnp.exp2((scores[u % 2, slot] - row_max) * scale).astype(jnp.bfloat16)
        values = v_refs[slot // groups][slot % groups, head * rows : (head + 1) * rows, :]
        return mixed + jnp.dot(
            weights, jnp.concatenate([values, ones], axis=1), preferred_element_type=jnp.float32
        )

    def queries(u):
        i, head = units[u]
        return q_refs[i][head * rows : (head + 1) * rows, :]

    top, q = lowest, queries(0)
    for slot in range(slots):
        top = score(0, slot, top, q)
    for u, (i, head) in enumerate(units):
        row_max = jnp.max(top, axis=1, keepdims=True)
        mixed, top = jnp.zeros((rows, 2 * HEAD_DIM), jnp.float32), lowest
        if u + 1 < len(units):
            q = queries(u + 1)
        for slot in range(slots):
            if u + 1 < len(units):
                top = score(u + 1, slot, top, q)
            mixed = weigh(u, slot, row_max, mixed)
        outs[i][head * rows : (head + 1) * rows, :] = (
            mixed[:, :HEAD_DIM] / mixed[:, HEAD_DIM : HEAD_DIM + 1]
        ).astype(jnp.bfloat16)


def collect_kernel(place_ref, *refs, count):
    out = refs[-1]
    rows = out.shape[0]
    for step in range(count):

        @pl.when(pl.program_id(0) == step)
        def _():
            for head in range(out.shape[1] // HEAD_DIM):
                piece = refs[step][head * rows : (head + 1) * rows, :]
                out[:, head * HEAD_DIM : (head + 1) * HEAD_DIM] = piece.astype(jnp.float32)


def exchanged(q_in, k_in, v_in, q_gain, k_gain, frames, adjacent, *, groups):
    rows, width = q_in.shape
    devices = lax.axis_size("seq")
    tensors = lax.axis_size("tensor")
    layers = devices // groups
    blk = rows // BLOCK
    blocks = devices * blk
    per_group = width // HEAD_DIM // groups
    me = lax.axis_index("seq")
    place, spot = me // layers, lax.rem(me, layers)
    place_row = place.reshape(1).astype(jnp.int32)
    f32, bf16 = jnp.float32, jnp.bfloat16
    params = pltpu.CompilerParams(vmem_limit_bytes=20 * MIB)
    def rotated(x, shift):
        pairs = [
            (z * layers + r, (z + shift) % groups * layers + r)
            for z in range(groups)
            for r in range(layers)
        ]
        return lax.ppermute(x, "seq", pairs)

    def exchange(pieces, after=None):
        shifts = range(1, groups)
        arrived = list(pieces)
        for s in shifts:
            if after is not None:
                arrived[s], after[s] = lax.optimization_barrier((arrived[s], after[s]))
            arrived[s] = rotated(arrived[s], s)
        return arrived

    def swapped(x, bit):
        return lax.ppermute(x, "seq", [(i, i ^ bit) for i in range(devices)])

    own_frames = lax.dynamic_slice_in_dim(frames, me * blk, blk, 0)
    gap = jnp.abs(own_frames[:, None] - frames[None, :])
    allowed = ((gap == 0) | (gap == 1) & (adjacent == 1)).astype(bf16)
    mask_rows = jnp.pad(allowed, ((0, MASK_ROWS - blk), (0, BLOCK - blocks)))

    v_pieces = pl.pallas_call(
        functools.partial(value_kernel, per_group=per_group),
        out_shape=[jax.ShapeDtypeStruct((per_group * rows, HEAD_DIM), bf16)] * groups,
        in_specs=[SMEM, VMEM],
        out_specs=[VMEM] * groups,
        compiler_params=params,
        name="value_pieces",
    )(place_row, v_in)
    q_in, k_in, v_pieces = lax.optimization_barrier((q_in, k_in, v_pieces))
    sums = pl.pallas_call(
        square_sums_kernel,
        out_shape=jax.ShapeDtypeStruct((rows, 2), f32),
        in_specs=[VMEM, VMEM],
        out_specs=VMEM,
        compiler_params=params,
        name="square_sums",
    )(q_in, k_in)
    v_arrived = exchange(v_pieces)
    sums = lax.psum(sums, "tensor")

    piece = jax.ShapeDtypeStruct((per_group * rows, HEAD_DIM), bf16)
    masked_piece = jax.ShapeDtypeStruct((per_group * rows + MASK_ROWS, HEAD_DIM), bf16)
    pieces = pl.pallas_call(
        functools.partial(
            norm_kernel, per_group=per_group, full_width=float(width * tensors)
        ),
        out_shape=[masked_piece] * groups + [piece] * groups,
        in_specs=[SMEM] + [VMEM] * 6,
        out_specs=[VMEM] * (2 * groups),
        compiler_params=params,
        name="norm_pieces",
    )(place_row, sums, q_in, k_in, q_gain.reshape(1, width), k_gain.reshape(1, width), mask_rows)
    k_arrived = exchange(pieces[:groups], v_arrived)
    v_stack = jnp.stack(v_arrived)
    q_arrived = exchange(pieces[groups:], k_arrived)

    low = per_group * rows
    known = jnp.stack([x[low : low + blk, :blocks] for x in k_arrived]).astype(f32)
    z_order = lax.rem(place - jnp.arange(groups) + groups, groups)
    layer_order = jnp.bitwise_xor(spot, jnp.arange(layers))
    key_blocks = (
        (z_order[None, :, None] * layers + layer_order[:, None, None]) * blk
        + jnp.arange(blk)[None, None, :]
    ).reshape(-1)
    key_hot = (key_blocks[:, None] == jnp.arange(blocks)[None, :]).astype(f32)
    table = jnp.einsum("gab,kb->gak", known, key_hot).reshape(groups, blk, devices, blk)
    bias = jnp.where(table > 0.5, 0.0, blocked).astype(f32).transpose(0, 2, 1, 3).reshape(-1)

    def spread(parts, bit):
        return parts | {have ^ bit: swapped(part, bit) for have, part in parts.items()}

    bits = [1 << i for i in reversed(range(layers.bit_length() - 1))]
    values, keys = {0: v_stack}, {}
    for bit in bits:
        values = spread(values, bit)
        if bit == bits[0]:
            k_arrived, values = lax.optimization_barrier((k_arrived, values))
            keys = {0: jnp.stack([x[: per_group * rows] for x in k_arrived])}
    for bit in bits:
        keys = spread(keys, bit)
        if bit == bits[0]:
            q_arrived, keys, bias = lax.optimization_barrier((q_arrived, keys, bias))
    values = [values[i] for i in range(layers)]
    keys = [keys[i] for i in range(layers)]

    scale = math.log2(math.e) / math.sqrt(HEAD_DIM)
    def attend(query_slots, bias):
        return pl.pallas_call(
            functools.partial(
                attend_kernel,
                query_slots=query_slots,
                groups=groups,
                layers=layers,
                heads=per_group,
                scale=scale,
            ),
            in_specs=[SMEM] + [VMEM] * (len(query_slots) + 2 * layers),
            out_specs=[VMEM] * len(query_slots),
            scratch_shapes=[pltpu.VMEM((2, devices, rows, rows), f32)],
            out_shape=[jax.ShapeDtypeStruct((per_group * rows, HEAD_DIM), bf16)] * len(query_slots),
            compiler_params=params,
            name="attend_" + "_".join(str(g) for g in query_slots),
        )(bias, *[q_arrived[g] for g in query_slots], *keys, *values)

    outputs = [None] * groups
    far = groups // 2
    near = tuple(g for g in range(1, groups) if g != far)
    for query_slots in ((far,), near, (0,)):
        if query_slots == (0,):
            outputs[far], bias = lax.optimization_barrier((outputs[far], bias))
        own = attend(query_slots, bias)
        own, bias = lax.optimization_barrier((own, bias))
        for g, x in zip(query_slots, own):
            outputs[g] = rotated(x, groups - g) if g else x

    def collect(shifts, base):
        def columns(step, place_ref):
            shift = shifts[-1]
            for i in reversed(range(len(shifts) - 1)):
                shift = jnp.where(step == i, shifts[i], shift)
            return 0, lax.rem(place_ref[0] + shift, groups)

        return pl.pallas_call(
            functools.partial(collect_kernel, count=len(shifts)),
            grid_spec=pltpu.PrefetchScalarGridSpec(
                num_scalar_prefetch=1,
                grid=(len(shifts),),
                in_specs=[VMEM] * len(shifts) + [ANY] * len(base),
                out_specs=pl.BlockSpec((rows, width // groups), columns),
            ),
            out_shape=jax.ShapeDtypeStruct((rows, width), f32),
            input_output_aliases={1 + len(shifts): 0} if base else {},
            compiler_params=params,
            name=f"collect_{shifts[0]}",
        )(place_row, *[outputs[g] for g in shifts], *base)

    return collect(near, [collect((0, far), [])])


def normalized(inputs, gain_row, square_sum, full_width):
    return (inputs / jnp.sqrt(square_sum / full_width + epsilon)[:, None] * gain_row).astype(
        jnp.bfloat16
    )


def shards(q_in, k_in, v_in, q_gain, k_gain, frames, adjacent):
    tok_rows = q_in.shape[0]
    width_dev = q_in.shape[1]
    full_width = width_dev * lax.axis_size("tensor")
    q_sum, k_sum = lax.psum((jnp.sum(q_in * q_in, axis=1), jnp.sum(k_in * k_in, axis=1)), "tensor")
    q_norm = normalized(q_in, q_gain, q_sum, full_width)
    k_norm = normalized(k_in, k_gain, k_sum, full_width)
    blk_dev = tok_rows // BLOCK
    device = lax.axis_index("seq")
    first_block = device * blk_dev
    query_frames = lax.dynamic_slice_in_dim(frames, first_block, blk_dev, 0)
    score_scale = 1.0 / math.sqrt(HEAD_DIM)
    head_count = width_dev // HEAD_DIM
    q_three = q_norm.reshape(tok_rows, head_count, HEAD_DIM)

    def masked_scores(key_rows, key_start):
        key_block = key_start // BLOCK
        key_frames = lax.dynamic_slice_in_dim(frames, key_block, blk_dev, 0)
        adjacent_rows = lax.dynamic_slice_in_dim(adjacent, key_block, blk_dev, 1)
        frame_gap = jnp.abs(query_frames[:, None] - key_frames[None, :])
        allowed_here = (frame_gap == 0) | (frame_gap == 1) & (adjacent_rows == 1)
        key_three = key_rows.reshape(tok_rows, head_count, HEAD_DIM)
        raw_scores = (
            jnp.einsum("thd,uhd->htu", q_three, key_three, preferred_element_type=jnp.float32)
            * score_scale
        )
        tiled_scores = raw_scores.reshape(head_count, blk_dev, BLOCK, blk_dev, BLOCK)
        tiled_scores = jnp.where(allowed_here[None, :, None, :, None], tiled_scores, blocked)
        return tiled_scores.reshape(head_count, tok_rows, tok_rows)

    piece = lax.all_gather(k_norm, "seq", axis=0, tiled=True)
    shard_count = piece.shape[0] // tok_rows

    def one_shard(shard, current):
        key_rows = lax.dynamic_slice_in_dim(piece, shard * tok_rows, tok_rows, 0)
        return jnp.maximum(current, jnp.max(masked_scores(key_rows, shard * tok_rows), axis=2))

    row_max = lax.fori_loop(
        0, shard_count, one_shard, jnp.full((head_count, tok_rows), blocked, jnp.float32)
    )
    start_sums = (
        jnp.zeros((head_count, tok_rows), jnp.float32),
        jnp.zeros((tok_rows, head_count, HEAD_DIM), jnp.float32),
    )
    key_piece = lax.all_gather(k_norm, "seq", axis=0, tiled=True)
    value_piece = lax.all_gather(v_in, "seq", axis=0, tiled=True)
    shard_count = key_piece.shape[0] // tok_rows

    def one_shard(shard, current):
        totals, accumulated = current
        key_rows = lax.dynamic_slice_in_dim(key_piece, shard * tok_rows, tok_rows, 0)
        value_rows = lax.dynamic_slice_in_dim(value_piece, shard * tok_rows, tok_rows, 0).reshape(
            tok_rows, head_count, HEAD_DIM
        )
        weights = jnp.exp(masked_scores(key_rows, shard * tok_rows) - row_max[:, :, None])
        totals = totals + jnp.sum(weights, axis=2)
        accumulated = accumulated + jnp.einsum(
            "htu,uhd->thd",
            weights.astype(jnp.bfloat16),
            value_rows,
            preferred_element_type=jnp.float32,
        )
        return (totals, accumulated)

    totals, accumulated = lax.fori_loop(0, shard_count, one_shard, start_sums)
    return (accumulated / totals.T[:, :, None]).reshape(tok_rows, width_dev)


def groups_of(mesh, heads):
    layers = 4
    groups = mesh.shape["seq"] // layers
    fits = groups & (groups - 1) == 0 and mesh.shape["seq"] == groups * layers
    fits = fits and heads % groups == 0 and heads >= 3 * groups
    return groups if fits else 1


def solution(mesh):
    def step(q_in, k_in, v_in, q_gain, k_gain, frames, adjacent):
        heads = q_in.shape[1] // mesh.shape["tensor"] // HEAD_DIM
        groups = groups_of(mesh, heads)
        body = shards if groups == 1 else functools.partial(exchanged, groups=groups)
        return jax.shard_map(
            body,
            mesh=mesh,
            in_specs=(
                P("seq", "tensor"),
                P("seq", "tensor"),
                P("seq", "tensor"),
                P("tensor"),
                P("tensor"),
                P(),
                P("seq", None),
            ),
            out_specs=P("seq", "tensor"),
            check_vma=False,
        )(q_in, k_in, v_in, q_gain, k_gain, frames, adjacent)

    return step
```

```python
import functools
import math

import jax
import jax.numpy as jnp
from jax import lax
from jax.experimental import pallas as pl
from jax.experimental.pallas import tpu as pltpu
from jax.sharding import PartitionSpec as P

HEAD_DIM = 128
BLOCK = 128
epsilon = 1e-06
blocked = -1e30
MASK_ROWS = 16
MIB = 1024 * 1024
VMEM = pl.BlockSpec(memory_space=pltpu.VMEM)
SMEM = pl.BlockSpec(memory_space=pltpu.SMEM)
ANY = pl.BlockSpec(memory_space=pl.ANY)


def column_of(place_ref, shift, head, groups, per_group):
    group = lax.rem(place_ref[0] + shift, groups)
    return pl.multiple_of((group * per_group + head) * HEAD_DIM, HEAD_DIM)


def value_kernel(place_ref, v_ref, *outs, per_group):
    groups = len(outs)
    rows = v_ref.shape[0]
    for shift, out in enumerate(outs):
        for head in range(per_group):
            column = column_of(place_ref, shift, head, groups, per_group)
            out[head * rows : (head + 1) * rows, :] = v_ref[:, pl.ds(column, HEAD_DIM)]


def square_sums_kernel(q_ref, k_ref, out_ref):
    q, k = q_ref[...], k_ref[...]
    out_ref[:, 0:1] = jnp.sum(q * q, axis=1, keepdims=True)
    out_ref[:, 1:2] = jnp.sum(k * k, axis=1, keepdims=True)


def normed_columns(x_ref, inverse, gain_ref, column):
    here = pl.ds(column, HEAD_DIM)
    return (x_ref[:, here] * inverse * gain_ref[:, here]).astype(jnp.bfloat16)


def norm_kernel(
    place_ref, sums_ref, q_ref, k_ref, q_gain_ref, k_gain_ref, mask_ref, *outs, per_group, full_width
):
    groups = len(outs) // 2
    rows = k_ref.shape[0]
    inverse = 1.0 / jnp.sqrt(sums_ref[...] / full_width + epsilon)
    for shift in range(groups):
        k_out, q_out = outs[shift], outs[groups + shift]
        for head in range(per_group):
            column = column_of(place_ref, shift, head, groups, per_group)
            q_out[head * rows : (head + 1) * rows, :] = normed_columns(
                q_ref, inverse[:, 0:1], q_gain_ref, column
            )
            k = normed_columns(k_ref, inverse[:, 1:2], k_gain_ref, column)
            for b in range(rows // BLOCK):
                low = head * rows + b * HEAD_DIM
                k_out[low : low + HEAD_DIM, :] = k[b * BLOCK : (b + 1) * BLOCK].T
        k_out[per_group * rows :, :] = mask_ref[...]


def attend_kernel(bias_ref, *refs, query_slots, groups, layers, heads, scale):
    count = len(query_slots)
    q_refs, refs = refs[:count], refs[count:]
    k_refs, v_refs = refs[:layers], refs[layers : 2 * layers]
    outs, scores = refs[2 * layers : -1], refs[-1]
    rows = outs[0].shape[0] // heads
    blk = rows // BLOCK
    slots = groups * layers
    lowest = jnp.full((rows, BLOCK), blocked, jnp.float32)
    ones = jnp.ones((rows, HEAD_DIM), jnp.bfloat16)
    units = [(i, head) for head in range(heads) for i in range(count)]

    def score(u, slot, top, q):
        i, head = units[u]
        keys = k_refs[slot // groups][slot % groups, head * rows : (head + 1) * rows, :]
        wide = jnp.concatenate(
            [keys[b * HEAD_DIM : (b + 1) * HEAD_DIM] for b in range(blk)], axis=1
        )
        products = jnp.dot(q, wide, preferred_element_type=jnp.float32)
        first = (query_slots[i] * slots + slot) * blk
        for b in range(blk):
            columns = slice(b * BLOCK, (b + 1) * BLOCK)
            block = jnp.concatenate(
                [
                    products[a * BLOCK : (a + 1) * BLOCK, columns] + bias_ref[(first + a) * blk + b]
                    for a in range(blk)
                ],
                axis=0,
            )
            scores[u % 2, slot, :, columns] = block
            top = jnp.maximum(top, block)
        return top

    def weigh(u, slot, row_max, mixed):
        head = units[u][1]
        weights = jnp.exp2((scores[u % 2, slot] - row_max) * scale).astype(jnp.bfloat16)
        values = v_refs[slot // groups][slot % groups, head * rows : (head + 1) * rows, :]
        return mixed + jnp.dot(
            weights, jnp.concatenate([values, ones], axis=1), preferred_element_type=jnp.float32
        )

    def queries(u):
        i, head = units[u]
        return q_refs[i][head * rows : (head + 1) * rows, :]

    top, q = lowest, queries(0)
    for slot in range(slots):
        top = score(0, slot, top, q)
    for u, (i, head) in enumerate(units):
        row_max = jnp.max(top, axis=1, keepdims=True)
        mixed, top = jnp.zeros((rows, 2 * HEAD_DIM), jnp.float32), lowest
        if u + 1 < len(units):
            q = queries(u + 1)
        for slot in range(slots):
            if u + 1 < len(units):
                top = score(u + 1, slot, top, q)
            mixed = weigh(u, slot, row_max, mixed)
        outs[i][head * rows : (head + 1) * rows, :] = (
            mixed[:, :HEAD_DIM] / mixed[:, HEAD_DIM : HEAD_DIM + 1]
        ).astype(jnp.bfloat16)


def collect_kernel(place_ref, *refs, count):
    out = refs[-1]
    rows = out.shape[0]
    for step in range(count):

        @pl.when(pl.program_id(0) == step)
        def _():
            for head in range(out.shape[1] // HEAD_DIM):
                piece = refs[step][head * rows : (head + 1) * rows, :]
                out[:, head * HEAD_DIM : (head + 1) * HEAD_DIM] = piece.astype(jnp.float32)


def exchanged(q_in, k_in, v_in, q_gain, k_gain, frames, adjacent, *, groups):
    rows, width = q_in.shape
    devices = lax.axis_size("seq")
    tensors = lax.axis_size("tensor")
    layers = devices // groups
    blk = rows // BLOCK
    blocks = devices * blk
    per_group = width // HEAD_DIM // groups
    me = lax.axis_index("seq")
    place, spot = me // layers, lax.rem(me, layers)
    place_row = place.reshape(1).astype(jnp.int32)
    f32, bf16 = jnp.float32, jnp.bfloat16
    params = pltpu.CompilerParams(vmem_limit_bytes=20 * MIB)
    def rotated(x, shift):
        pairs = [
            (z * layers + r, (z + shift) % groups * layers + r)
            for z in range(groups)
            for r in range(layers)
        ]
        return lax.ppermute(x, "seq", pairs)

    def exchange(pieces, after=None):
        shifts = range(1, groups)
        arrived = list(pieces)
        for s in shifts:
            if after is not None:
                arrived[s], after[s] = lax.optimization_barrier((arrived[s], after[s]))
            arrived[s] = rotated(arrived[s], s)
        return arrived

    def swapped(x, bit):
        return lax.ppermute(x, "seq", [(i, i ^ bit) for i in range(devices)])

    own_frames = lax.dynamic_slice_in_dim(frames, me * blk, blk, 0)
    gap = jnp.abs(own_frames[:, None] - frames[None, :])
    allowed = ((gap == 0) | (gap == 1) & (adjacent == 1)).astype(bf16)
    mask_rows = jnp.pad(allowed, ((0, MASK_ROWS - blk), (0, BLOCK - blocks)))

    v_pieces = pl.pallas_call(
        functools.partial(value_kernel, per_group=per_group),
        out_shape=[jax.ShapeDtypeStruct((per_group * rows, HEAD_DIM), bf16)] * groups,
        in_specs=[SMEM, VMEM],
        out_specs=[VMEM] * groups,
        compiler_params=params,
        name="value_pieces",
    )(place_row, v_in)
    q_in, k_in, v_pieces = lax.optimization_barrier((q_in, k_in, v_pieces))
    sums = pl.pallas_call(
        square_sums_kernel,
        out_shape=jax.ShapeDtypeStruct((rows, 2), f32),
        in_specs=[VMEM, VMEM],
        out_specs=VMEM,
        compiler_params=params,
        name="square_sums",
    )(q_in, k_in)
    v_arrived = exchange(v_pieces)
    sums = lax.psum(sums, "tensor")

    piece = jax.ShapeDtypeStruct((per_group * rows, HEAD_DIM), bf16)
    masked_piece = jax.ShapeDtypeStruct((per_group * rows + MASK_ROWS, HEAD_DIM), bf16)
    pieces = pl.pallas_call(
        functools.partial(
            norm_kernel, per_group=per_group, full_width=float(width * tensors)
        ),
        out_shape=[masked_piece] * groups + [piece] * groups,
        in_specs=[SMEM] + [VMEM] * 6,
        out_specs=[VMEM] * (2 * groups),
        compiler_params=params,
        name="norm_pieces",
    )(place_row, sums, q_in, k_in, q_gain.reshape(1, width), k_gain.reshape(1, width), mask_rows)
    k_arrived = exchange(pieces[:groups], v_arrived)
    v_stack = jnp.stack(v_arrived)
    q_arrived = exchange(pieces[groups:], [k_arrived[groups - 1]] * groups)

    low = per_group * rows
    known = jnp.stack([x[low : low + blk, :blocks] for x in k_arrived]).astype(f32)
    z_order = lax.rem(place - jnp.arange(groups) + groups, groups)
    layer_order = jnp.bitwise_xor(spot, jnp.arange(layers))
    key_blocks = (
        (z_order[None, :, None] * layers + layer_order[:, None, None]) * blk
        + jnp.arange(blk)[None, None, :]
    ).reshape(-1)
    key_hot = (key_blocks[:, None] == jnp.arange(blocks)[None, :]).astype(f32)
    table = jnp.einsum("gab,kb->gak", known, key_hot).reshape(groups, blk, devices, blk)
    bias = jnp.where(table > 0.5, 0.0, blocked).astype(f32).transpose(0, 2, 1, 3).reshape(-1)

    def spread(parts, bit):
        return parts | {have ^ bit: swapped(part, bit) for have, part in parts.items()}

    bits = [1 << i for i in reversed(range(layers.bit_length() - 1))]
    values, keys = {0: v_stack}, {}
    for bit in bits:
        values = spread(values, bit)
        if bit == bits[0]:
            k_arrived, values = lax.optimization_barrier((k_arrived, values))
            keys = {0: jnp.stack([x[: per_group * rows] for x in k_arrived])}
    for bit in bits:
        keys = spread(keys, bit)
        if bit == bits[0]:
            q_arrived, keys, bias = lax.optimization_barrier((q_arrived, keys, bias))
    values = [values[i] for i in range(layers)]
    keys = [keys[i] for i in range(layers)]

    scale = math.log2(math.e) / math.sqrt(HEAD_DIM)
    def attend(query_slots, bias):
        return pl.pallas_call(
            functools.partial(
                attend_kernel,
                query_slots=query_slots,
                groups=groups,
                layers=layers,
                heads=per_group,
                scale=scale,
            ),
            in_specs=[SMEM] + [VMEM] * (len(query_slots) + 2 * layers),
            out_specs=[VMEM] * len(query_slots),
            scratch_shapes=[pltpu.VMEM((2, devices, rows, rows), f32)],
            out_shape=[jax.ShapeDtypeStruct((per_group * rows, HEAD_DIM), bf16)] * len(query_slots),
            compiler_params=params,
            name="attend_" + "_".join(str(g) for g in query_slots),
        )(bias, *[q_arrived[g] for g in query_slots], *keys, *values)

    outputs = [None] * groups
    far = groups // 2
    near = tuple(g for g in range(1, groups) if g != far)
    for query_slots in ((far,), near, (0,)):
        if query_slots == (0,):
            outputs[far], bias = lax.optimization_barrier((outputs[far], bias))
        own = attend(query_slots, bias)
        own, bias = lax.optimization_barrier((own, bias))
        for g, x in zip(query_slots, own):
            outputs[g] = rotated(x, groups - g) if g else x

    def collect(shifts, base):
        def columns(step, place_ref):
            shift = shifts[-1]
            for i in reversed(range(len(shifts) - 1)):
                shift = jnp.where(step == i, shifts[i], shift)
            return 0, lax.rem(place_ref[0] + shift, groups)

        return pl.pallas_call(
            functools.partial(collect_kernel, count=len(shifts)),
            grid_spec=pltpu.PrefetchScalarGridSpec(
                num_scalar_prefetch=1,
                grid=(len(shifts),),
                in_specs=[VMEM] * len(shifts) + [ANY] * len(base),
                out_specs=pl.BlockSpec((rows, width // groups), columns),
            ),
            out_shape=jax.ShapeDtypeStruct((rows, width), f32),
            input_output_aliases={1 + len(shifts): 0} if base else {},
            compiler_params=params,
            name=f"collect_{shifts[0]}",
        )(place_row, *[outputs[g] for g in shifts], *base)

    return collect(near, [collect((0, far), [])])


def normalized(inputs, gain_row, square_sum, full_width):
    return (inputs / jnp.sqrt(square_sum / full_width + epsilon)[:, None] * gain_row).astype(
        jnp.bfloat16
    )


def shards(q_in, k_in, v_in, q_gain, k_gain, frames, adjacent):
    tok_rows = q_in.shape[0]
    width_dev = q_in.shape[1]
    full_width = width_dev * lax.axis_size("tensor")
    q_sum, k_sum = lax.psum((jnp.sum(q_in * q_in, axis=1), jnp.sum(k_in * k_in, axis=1)), "tensor")
    q_norm = normalized(q_in, q_gain, q_sum, full_width)
    k_norm = normalized(k_in, k_gain, k_sum, full_width)
    blk_dev = tok_rows // BLOCK
    device = lax.axis_index("seq")
    first_block = device * blk_dev
    query_frames = lax.dynamic_slice_in_dim(frames, first_block, blk_dev, 0)
    score_scale = 1.0 / math.sqrt(HEAD_DIM)
    head_count = width_dev // HEAD_DIM
    q_three = q_norm.reshape(tok_rows, head_count, HEAD_DIM)

    def masked_scores(key_rows, key_start):
        key_block = key_start // BLOCK
        key_frames = lax.dynamic_slice_in_dim(frames, key_block, blk_dev, 0)
        adjacent_rows = lax.dynamic_slice_in_dim(adjacent, key_block, blk_dev, 1)
        frame_gap = jnp.abs(query_frames[:, None] - key_frames[None, :])
        allowed_here = (frame_gap == 0) | (frame_gap == 1) & (adjacent_rows == 1)
        key_three = key_rows.reshape(tok_rows, head_count, HEAD_DIM)
        raw_scores = (
            jnp.einsum("thd,uhd->htu", q_three, key_three, preferred_element_type=jnp.float32)
            * score_scale
        )
        tiled_scores = raw_scores.reshape(head_count, blk_dev, BLOCK, blk_dev, BLOCK)
        tiled_scores = jnp.where(allowed_here[None, :, None, :, None], tiled_scores, blocked)
        return tiled_scores.reshape(head_count, tok_rows, tok_rows)

    piece = lax.all_gather(k_norm, "seq", axis=0, tiled=True)
    shard_count = piece.shape[0] // tok_rows

    def one_shard(shard, current):
        key_rows = lax.dynamic_slice_in_dim(piece, shard * tok_rows, tok_rows, 0)
        return jnp.maximum(current, jnp.max(masked_scores(key_rows, shard * tok_rows), axis=2))

    row_max = lax.fori_loop(
        0, shard_count, one_shard, jnp.full((head_count, tok_rows), blocked, jnp.float32)
    )
    start_sums = (
        jnp.zeros((head_count, tok_rows), jnp.float32),
        jnp.zeros((tok_rows, head_count, HEAD_DIM), jnp.float32),
    )
    key_piece = lax.all_gather(k_norm, "seq", axis=0, tiled=True)
    value_piece = lax.all_gather(v_in, "seq", axis=0, tiled=True)
    shard_count = key_piece.shape[0] // tok_rows

    def one_shard(shard, current):
        totals, accumulated = current
        key_rows = lax.dynamic_slice_in_dim(key_piece, shard * tok_rows, tok_rows, 0)
        value_rows = lax.dynamic_slice_in_dim(value_piece, shard * tok_rows, tok_rows, 0).reshape(
            tok_rows, head_count, HEAD_DIM
        )
        weights = jnp.exp(masked_scores(key_rows, shard * tok_rows) - row_max[:, :, None])
        totals = totals + jnp.sum(weights, axis=2)
        accumulated = accumulated + jnp.einsum(
            "htu,uhd->thd",
            weights.astype(jnp.bfloat16),
            value_rows,
            preferred_element_type=jnp.float32,
        )
        return (totals, accumulated)

    totals, accumulated = lax.fori_loop(0, shard_count, one_shard, start_sums)
    return (accumulated / totals.T[:, :, None]).reshape(tok_rows, width_dev)


def groups_of(mesh, heads):
    layers = 4
    groups = mesh.shape["seq"] // layers
    fits = groups & (groups - 1) == 0 and mesh.shape["seq"] == groups * layers
    fits = fits and heads % groups == 0 and heads >= 3 * groups
    return groups if fits else 1


def solution(mesh):
    def step(q_in, k_in, v_in, q_gain, k_gain, frames, adjacent):
        heads = q_in.shape[1] // mesh.shape["tensor"] // HEAD_DIM
        groups = groups_of(mesh, heads)
        body = shards if groups == 1 else functools.partial(exchanged, groups=groups)
        return jax.shard_map(
            body,
            mesh=mesh,
            in_specs=(
                P("seq", "tensor"),
                P("seq", "tensor"),
                P("seq", "tensor"),
                P("tensor"),
                P("tensor"),
                P(),
                P("seq", None),
            ),
            out_specs=P("seq", "tensor"),
            check_vma=False,
        )(q_in, k_in, v_in, q_gain, k_gain, frames, adjacent)

    return step
```

```python
import functools
import math

import jax
import jax.numpy as jnp
from jax import lax
from jax.experimental import pallas as pl
from jax.experimental.pallas import tpu as pltpu
from jax.sharding import PartitionSpec as P

HEAD_DIM = 128
BLOCK = 128
epsilon = 1e-06
blocked = -1e30
MASK_ROWS = 16
MIB = 1024 * 1024
VMEM = pl.BlockSpec(memory_space=pltpu.VMEM)
SMEM = pl.BlockSpec(memory_space=pltpu.SMEM)
ANY = pl.BlockSpec(memory_space=pl.ANY)


def column_of(place_ref, shift, head, groups, per_group):
    group = lax.rem(place_ref[0] + shift, groups)
    return pl.multiple_of((group * per_group + head) * HEAD_DIM, HEAD_DIM)


def value_kernel(place_ref, v_ref, *refs, per_group):
    outs, semaphores = refs[:-1], refs[-1]
    rows = v_ref.shape[0]
    copies = []
    for shift, out in enumerate(outs):
        for head in range(per_group):
            column = column_of(place_ref, shift, head, len(outs), per_group)
            copies.append(
                pltpu.make_async_copy(
                    v_ref.at[:, pl.ds(column, HEAD_DIM)],
                    out.at[pl.ds(head * rows, rows), :],
                    semaphores.at[len(copies)],
                )
            )
    for copy in copies:
        copy.start()
    for copy in copies:
        copy.wait()


def square_sums_kernel(q_ref, k_ref, out_ref):
    q, k = q_ref[...], k_ref[...]
    out_ref[:, 0:1] = jnp.sum(q * q, axis=1, keepdims=True)
    out_ref[:, 1:2] = jnp.sum(k * k, axis=1, keepdims=True)


def normed_columns(x_ref, inverse, gain_ref, column):
    here = pl.ds(column, HEAD_DIM)
    return (x_ref[:, here] * inverse * gain_ref[:, here]).astype(jnp.bfloat16)


def norm_kernel(
    place_ref, sums_ref, q_ref, k_ref, q_gain_ref, k_gain_ref, mask_ref, *outs, per_group, full_width
):
    groups = len(outs) // 2
    rows = k_ref.shape[0]
    inverse = 1.0 / jnp.sqrt(sums_ref[...] / full_width + epsilon)
    for shift in range(groups):
        k_out, q_out = outs[shift], outs[groups + shift]
        for head in range(per_group):
            column = column_of(place_ref, shift, head, groups, per_group)
            q_out[head * rows : (head + 1) * rows, :] = normed_columns(
                q_ref, inverse[:, 0:1], q_gain_ref, column
            )
            k = normed_columns(k_ref, inverse[:, 1:2], k_gain_ref, column)
            for b in range(rows // BLOCK):
                low = head * rows + b * HEAD_DIM
                k_out[low : low + HEAD_DIM, :] = k[b * BLOCK : (b + 1) * BLOCK].T
        k_out[per_group * rows :, :] = mask_ref[...]


def attend_kernel(bias_ref, *refs, query_slots, groups, layers, heads, scale):
    count = len(query_slots)
    q_refs, refs = refs[:count], refs[count:]
    k_refs, v_refs = refs[:layers], refs[layers : 2 * layers]
    outs, scores = refs[2 * layers : -1], refs[-1]
    rows = outs[0].shape[0] // heads
    blk = rows // BLOCK
    slots = groups * layers
    lowest = jnp.full((rows, BLOCK), blocked, jnp.float32)
    ones = jnp.ones((rows, HEAD_DIM), jnp.bfloat16)
    units = [(i, head) for head in range(heads) for i in range(count)]

    def score(u, slot, top, q):
        i, head = units[u]
        keys = k_refs[slot // groups][slot % groups, head * rows : (head + 1) * rows, :]
        wide = jnp.concatenate(
            [keys[b * HEAD_DIM : (b + 1) * HEAD_DIM] for b in range(blk)], axis=1
        )
        products = jnp.dot(q, wide, preferred_element_type=jnp.float32)
        first = (query_slots[i] * slots + slot) * blk
        for b in range(blk):
            columns = slice(b * BLOCK, (b + 1) * BLOCK)
            block = jnp.concatenate(
                [
                    products[a * BLOCK : (a + 1) * BLOCK, columns] + bias_ref[(first + a) * blk + b]
                    for a in range(blk)
                ],
                axis=0,
            )
            scores[u % 2, slot, :, columns] = block
            top = jnp.maximum(top, block)
        return top

    def weigh(u, slot, row_max, mixed):
        head = units[u][1]
        weights = jnp.exp2((scores[u % 2, slot] - row_max) * scale).astype(jnp.bfloat16)
        values = v_refs[slot // groups][slot % groups, head * rows : (head + 1) * rows, :]
        return mixed + jnp.dot(
            weights, jnp.concatenate([values, ones], axis=1), preferred_element_type=jnp.float32
        )

    def queries(u):
        i, head = units[u]
        return q_refs[i][head * rows : (head + 1) * rows, :]

    top, q = lowest, queries(0)
    for slot in range(slots):
        top = score(0, slot, top, q)
    for u, (i, head) in enumerate(units):
        row_max = jnp.max(top, axis=1, keepdims=True)
        mixed, top = jnp.zeros((rows, 2 * HEAD_DIM), jnp.float32), lowest
        if u + 1 < len(units):
            q = queries(u + 1)
        for slot in range(slots):
            if u + 1 < len(units):
                top = score(u + 1, slot, top, q)
            mixed = weigh(u, slot, row_max, mixed)
        outs[i][head * rows : (head + 1) * rows, :] = (
            mixed[:, :HEAD_DIM] / mixed[:, HEAD_DIM : HEAD_DIM + 1]
        ).astype(jnp.bfloat16)


def collect_kernel(place_ref, *refs, count):
    out = refs[-1]
    rows = out.shape[0]
    for step in range(count):

        @pl.when(pl.program_id(0) == step)
        def _():
            for head in range(out.shape[1] // HEAD_DIM):
                piece = refs[step][head * rows : (head + 1) * rows, :]
                out[:, head * HEAD_DIM : (head + 1) * HEAD_DIM] = piece.astype(jnp.float32)


def exchanged(q_in, k_in, v_in, q_gain, k_gain, frames, adjacent, *, groups):
    rows, width = q_in.shape
    devices = lax.axis_size("seq")
    tensors = lax.axis_size("tensor")
    layers = devices // groups
    blk = rows // BLOCK
    blocks = devices * blk
    per_group = width // HEAD_DIM // groups
    me = lax.axis_index("seq")
    place, spot = me // layers, lax.rem(me, layers)
    place_row = place.reshape(1).astype(jnp.int32)
    f32, bf16 = jnp.float32, jnp.bfloat16
    params = pltpu.CompilerParams(vmem_limit_bytes=20 * MIB)
    def rotated(x, shift):
        pairs = [
            (z * layers + r, (z + shift) % groups * layers + r)
            for z in range(groups)
            for r in range(layers)
        ]
        return lax.ppermute(x, "seq", pairs)

    def exchange(pieces, after=None):
        shifts = range(1, groups)
        arrived = list(pieces)
        for s in shifts:
            if after is not None:
                arrived[s], after[s] = lax.optimization_barrier((arrived[s], after[s]))
            arrived[s] = rotated(arrived[s], s)
        return arrived

    def swapped(x, bit):
        return lax.ppermute(x, "seq", [(i, i ^ bit) for i in range(devices)])

    own_frames = lax.dynamic_slice_in_dim(frames, me * blk, blk, 0)
    gap = jnp.abs(own_frames[:, None] - frames[None, :])
    allowed = ((gap == 0) | (gap == 1) & (adjacent == 1)).astype(bf16)
    mask_rows = jnp.pad(allowed, ((0, MASK_ROWS - blk), (0, BLOCK - blocks)))

    v_pieces = pl.pallas_call(
        functools.partial(value_kernel, per_group=per_group),
        out_shape=[jax.ShapeDtypeStruct((per_group * rows, HEAD_DIM), bf16)] * groups,
        in_specs=[SMEM, ANY],
        out_specs=[ANY] * groups,
        scratch_shapes=[pltpu.SemaphoreType.DMA((groups * per_group,))],
        compiler_params=params,
        name="value_pieces",
    )(place_row, v_in)
    q_in, k_in, v_pieces = lax.optimization_barrier((q_in, k_in, v_pieces))
    sums = pl.pallas_call(
        square_sums_kernel,
        out_shape=jax.ShapeDtypeStruct((rows, 2), f32),
        in_specs=[VMEM, VMEM],
        out_specs=VMEM,
        compiler_params=params,
        name="square_sums",
    )(q_in, k_in)
    v_arrived = exchange(v_pieces)
    sums = lax.psum(sums, "tensor")

    piece = jax.ShapeDtypeStruct((per_group * rows, HEAD_DIM), bf16)
    masked_piece = jax.ShapeDtypeStruct((per_group * rows + MASK_ROWS, HEAD_DIM), bf16)
    pieces = pl.pallas_call(
        functools.partial(
            norm_kernel, per_group=per_group, full_width=float(width * tensors)
        ),
        out_shape=[masked_piece] * groups + [piece] * groups,
        in_specs=[SMEM] + [VMEM] * 6,
        out_specs=[VMEM] * (2 * groups),
        compiler_params=params,
        name="norm_pieces",
    )(place_row, sums, q_in, k_in, q_gain.reshape(1, width), k_gain.reshape(1, width), mask_rows)
    k_arrived = exchange(pieces[:groups], v_arrived)
    v_stack = jnp.stack(v_arrived)
    q_arrived = exchange(pieces[groups:], [k_arrived[groups - 1]] * groups)

    low = per_group * rows
    known = jnp.stack([x[low : low + blk, :blocks] for x in k_arrived]).astype(f32)
    z_order = lax.rem(place - jnp.arange(groups) + groups, groups)
    layer_order = jnp.bitwise_xor(spot, jnp.arange(layers))
    key_blocks = (
        (z_order[None, :, None] * layers + layer_order[:, None, None]) * blk
        + jnp.arange(blk)[None, None, :]
    ).reshape(-1)
    key_hot = (key_blocks[:, None] == jnp.arange(blocks)[None, :]).astype(f32)
    table = jnp.einsum("gab,kb->gak", known, key_hot).reshape(groups, blk, devices, blk)
    bias = jnp.where(table > 0.5, 0.0, blocked).astype(f32).transpose(0, 2, 1, 3).reshape(-1)

    def spread(parts, bit):
        return parts | {have ^ bit: swapped(part, bit) for have, part in parts.items()}

    bits = [1 << i for i in reversed(range(layers.bit_length() - 1))]
    values, keys = {0: v_stack}, {}
    for bit in bits:
        values = spread(values, bit)
        if bit == bits[0]:
            k_arrived, values = lax.optimization_barrier((k_arrived, values))
            keys = {0: jnp.stack([x[: per_group * rows] for x in k_arrived])}
    for bit in bits:
        keys = spread(keys, bit)
        if bit == bits[0]:
            q_arrived, keys, bias = lax.optimization_barrier((q_arrived, keys, bias))
    values = [values[i] for i in range(layers)]
    keys = [keys[i] for i in range(layers)]

    scale = math.log2(math.e) / math.sqrt(HEAD_DIM)
    def attend(query_slots, bias):
        return pl.pallas_call(
            functools.partial(
                attend_kernel,
                query_slots=query_slots,
                groups=groups,
                layers=layers,
                heads=per_group,
                scale=scale,
            ),
            in_specs=[SMEM] + [VMEM] * (len(query_slots) + 2 * layers),
            out_specs=[VMEM] * len(query_slots),
            scratch_shapes=[pltpu.VMEM((2, devices, rows, rows), f32)],
            out_shape=[jax.ShapeDtypeStruct((per_group * rows, HEAD_DIM), bf16)] * len(query_slots),
            compiler_params=params,
            name="attend_" + "_".join(str(g) for g in query_slots),
        )(bias, *[q_arrived[g] for g in query_slots], *keys, *values)

    outputs = [None] * groups
    far = groups // 2
    near = tuple(g for g in range(1, groups) if g != far)
    for query_slots in ((far,), near, (0,)):
        if query_slots == (0,):
            outputs[far], bias = lax.optimization_barrier((outputs[far], bias))
        own = attend(query_slots, bias)
        own, bias = lax.optimization_barrier((own, bias))
        for g, x in zip(query_slots, own):
            outputs[g] = rotated(x, groups - g) if g else x

    def collect(shifts, base):
        def columns(step, place_ref):
            shift = shifts[-1]
            for i in reversed(range(len(shifts) - 1)):
                shift = jnp.where(step == i, shifts[i], shift)
            return 0, lax.rem(place_ref[0] + shift, groups)

        return pl.pallas_call(
            functools.partial(collect_kernel, count=len(shifts)),
            grid_spec=pltpu.PrefetchScalarGridSpec(
                num_scalar_prefetch=1,
                grid=(len(shifts),),
                in_specs=[VMEM] * len(shifts) + [ANY] * len(base),
                out_specs=pl.BlockSpec((rows, width // groups), columns),
            ),
            out_shape=jax.ShapeDtypeStruct((rows, width), f32),
            input_output_aliases={1 + len(shifts): 0} if base else {},
            compiler_params=params,
            name=f"collect_{shifts[0]}",
        )(place_row, *[outputs[g] for g in shifts], *base)

    return collect(near, [collect((0, far), [])])


def normalized(inputs, gain_row, square_sum, full_width):
    return (inputs / jnp.sqrt(square_sum / full_width + epsilon)[:, None] * gain_row).astype(
        jnp.bfloat16
    )


def shards(q_in, k_in, v_in, q_gain, k_gain, frames, adjacent):
    tok_rows = q_in.shape[0]
    width_dev = q_in.shape[1]
    full_width = width_dev * lax.axis_size("tensor")
    q_sum, k_sum = lax.psum((jnp.sum(q_in * q_in, axis=1), jnp.sum(k_in * k_in, axis=1)), "tensor")
    q_norm = normalized(q_in, q_gain, q_sum, full_width)
    k_norm = normalized(k_in, k_gain, k_sum, full_width)
    blk_dev = tok_rows // BLOCK
    device = lax.axis_index("seq")
    first_block = device * blk_dev
    query_frames = lax.dynamic_slice_in_dim(frames, first_block, blk_dev, 0)
    score_scale = 1.0 / math.sqrt(HEAD_DIM)
    head_count = width_dev // HEAD_DIM
    q_three = q_norm.reshape(tok_rows, head_count, HEAD_DIM)

    def masked_scores(key_rows, key_start):
        key_block = key_start // BLOCK
        key_frames = lax.dynamic_slice_in_dim(frames, key_block, blk_dev, 0)
        adjacent_rows = lax.dynamic_slice_in_dim(adjacent, key_block, blk_dev, 1)
        frame_gap = jnp.abs(query_frames[:, None] - key_frames[None, :])
        allowed_here = (frame_gap == 0) | (frame_gap == 1) & (adjacent_rows == 1)
        key_three = key_rows.reshape(tok_rows, head_count, HEAD_DIM)
        raw_scores = (
            jnp.einsum("thd,uhd->htu", q_three, key_three, preferred_element_type=jnp.float32)
            * score_scale
        )
        tiled_scores = raw_scores.reshape(head_count, blk_dev, BLOCK, blk_dev, BLOCK)
        tiled_scores = jnp.where(allowed_here[None, :, None, :, None], tiled_scores, blocked)
        return tiled_scores.reshape(head_count, tok_rows, tok_rows)

    piece = lax.all_gather(k_norm, "seq", axis=0, tiled=True)
    shard_count = piece.shape[0] // tok_rows

    def one_shard(shard, current):
        key_rows = lax.dynamic_slice_in_dim(piece, shard * tok_rows, tok_rows, 0)
        return jnp.maximum(current, jnp.max(masked_scores(key_rows, shard * tok_rows), axis=2))

    row_max = lax.fori_loop(
        0, shard_count, one_shard, jnp.full((head_count, tok_rows), blocked, jnp.float32)
    )
    start_sums = (
        jnp.zeros((head_count, tok_rows), jnp.float32),
        jnp.zeros((tok_rows, head_count, HEAD_DIM), jnp.float32),
    )
    key_piece = lax.all_gather(k_norm, "seq", axis=0, tiled=True)
    value_piece = lax.all_gather(v_in, "seq", axis=0, tiled=True)
    shard_count = key_piece.shape[0] // tok_rows

    def one_shard(shard, current):
        totals, accumulated = current
        key_rows = lax.dynamic_slice_in_dim(key_piece, shard * tok_rows, tok_rows, 0)
        value_rows = lax.dynamic_slice_in_dim(value_piece, shard * tok_rows, tok_rows, 0).reshape(
            tok_rows, head_count, HEAD_DIM
        )
        weights = jnp.exp(masked_scores(key_rows, shard * tok_rows) - row_max[:, :, None])
        totals = totals + jnp.sum(weights, axis=2)
        accumulated = accumulated + jnp.einsum(
            "htu,uhd->thd",
            weights.astype(jnp.bfloat16),
            value_rows,
            preferred_element_type=jnp.float32,
        )
        return (totals, accumulated)

    totals, accumulated = lax.fori_loop(0, shard_count, one_shard, start_sums)
    return (accumulated / totals.T[:, :, None]).reshape(tok_rows, width_dev)


def groups_of(mesh, heads):
    layers = 4
    groups = mesh.shape["seq"] // layers
    fits = groups & (groups - 1) == 0 and mesh.shape["seq"] == groups * layers
    fits = fits and heads % groups == 0 and heads >= 3 * groups
    return groups if fits else 1


def solution(mesh):
    def step(q_in, k_in, v_in, q_gain, k_gain, frames, adjacent):
        heads = q_in.shape[1] // mesh.shape["tensor"] // HEAD_DIM
        groups = groups_of(mesh, heads)
        body = shards if groups == 1 else functools.partial(exchanged, groups=groups)
        return jax.shard_map(
            body,
            mesh=mesh,
            in_specs=(
                P("seq", "tensor"),
                P("seq", "tensor"),
                P("seq", "tensor"),
                P("tensor"),
                P("tensor"),
                P(),
                P("seq", None),
            ),
            out_specs=P("seq", "tensor"),
            check_vma=False,
        )(q_in, k_in, v_in, q_gain, k_gain, frames, adjacent)

    return step
```
